32 devices in a mesh: dp: 8 (over z, y), tensor: 4 (over x, core).
Axes of the slice: x: 2, y: 2, z: 4, core: 2. Of those that a mesh axis runs over, the one named last changes fastest.
Arguments:
- hidden: bfloat16 [1536, 4096], P('dp'), may hold values from -64 to 64
- output_weight: bfloat16 [4096, 128256], P(None, ('dp', 'tensor')), may hold values from -0.109375 to 0.109375
- targets: int32 [1536], P('dp'), may hold values from 0 to 128255
- labels: int32 [1536, 1], P('dp'), may hold values from 0 to 63; in each aligned block of 192 rows (0 to 191, 192 to 383, ...) at most 12 rows name the same one
- prev_scores: float32 [64], P('dp'), may hold values from -12 to 320
- prev_probs: float32 [64], P('dp')
- next_domains: int32 [128], P('dp'), may hold values from 0 to 63
Outputs:
- token_loss: float32 [1536], P(('dp', 'tensor'))
- new_scores: float32 [64], P('dp')
- log_probs: float32 [64], replicated
- sample_weights: float32 [128], P('dp')
The draws below stay inside these ranges and needn't reach their ends.
Inputs may be any that keep to these rules, and one draw needn't show every extreme that they name: `labels`: within the 192 tokens of one index of dp no domain appears more than 12 times; every domain appears somewhere in the batch.
All inputs are finite; a program needn't handle non-finite values.
Results may differ from the reference program's by a relative error of at most 0.0003.
Values may be sent and summed in bfloat16 or wider, within the bound.
No kernel may reach another device: no remote copies, remote signals or barrier semaphores. Data moves between devices by JAX's collectives and lax.ppermute only.
A program may use at most 128 MiB of HBM per device.

```python
import math
import jax
import jax.numpy as jnp
import numpy as np
from jax import lax

D = 4096
V = 128256
K = 64
STEP = 2000
TOK_DEV = 192
CAP = 12
TOKENS = 1536
NEXT = 128


def weight_columns(key, columns):
    bound = 7.0 * D ** (-0.5)
    drawn = jax.vmap(lambda column: jax.random.normal(jax.random.fold_in(key, column), (D,), jnp.float32))(columns)
    return jnp.clip(drawn * D ** (-0.5), -bound, bound)


def draw_output_weight(key, part):
    columns = jnp.arange(V, dtype=jnp.int32)
    return weight_columns(jax.random.fold_in(key, 11), columns).T.astype(jnp.bfloat16)


def draw_hidden(key, part):
    index_rows = jnp.arange(TOKENS, dtype=jnp.int32)
    rising = 3.0 ** (index_rows.astype(jnp.float32) / TOKENS)
    base = jax.random.normal(jax.random.fold_in(key, 23), (TOKENS, D), jnp.float32)
    scales = 0.6 * rising * jnp.exp(jax.random.uniform(jax.random.fold_in(key, 29), (TOKENS,), jnp.float32, -0.35, 0.35))
    result = base * scales[:, None]
    return jnp.clip(result, -64.0, 64.0).astype(jnp.bfloat16)


def draw_prev_scores(key, part):
    noise = jax.random.normal(jax.random.fold_in(key, 41), (K,), jnp.float32)
    values = 2.0 * noise
    return jnp.clip(values, -12.0, 320.0)


def draw_prev_probs(key, part):
    earlier = min(1.0 / K, math.sqrt(math.log(K) / (K * (STEP - 1))))
    logits = 1.5 * jax.random.normal(jax.random.fold_in(key, 43), (K,), jnp.float32)
    return earlier + (1.0 - K * earlier) * jax.nn.softmax(logits)


def plant(values, stream_key, least, high):
    index_at = [jax.random.randint(jax.random.fold_in(stream_key, axis), (), 0, length) for axis, length in enumerate(values.shape)]
    widest = values.shape.index(max(values.shape))
    beside = index_at[:widest] + [(index_at[widest] + 1) % values.shape[widest]] + index_at[widest + 1:]
    return values.at[tuple(index_at)].set(least).at[tuple(beside)].set(high)


def shared_out(rng, own, number, rows, number_of, top, limit, skew):
    sequence = jax.random.permutation(rng, number_of)
    crowded, common = shares(number_of, rows * top, limit, skew, True), shares(number_of, rows * top, limit, skew, False)
    places = jnp.arange(number_of)

    def named(sizes, offset_by):
        used = int((sizes > 0).sum())
        fixed = max(1, used // 4)
        passed = fixed + (places - fixed + offset_by * (used - fixed)) % max(1, number_of - fixed)
        return jnp.zeros((number_of,), jnp.int32).at[sequence[jnp.where(places < fixed, places, passed)]].set(jnp.asarray(sizes, jnp.int32))

    sizes = jnp.where(number % 4 == 0, named(crowded, number // 4), named(common, number - number // 4 - 1))
    mixed = jax.random.permutation(jax.random.fold_in(own, 3), number_of)
    source_of, taker = mixed[0:number_of // 2 * 2:2], mixed[1:number_of // 2 * 2:2]
    margin = jnp.minimum(sizes[source_of] - 1, limit - sizes[taker]) // 2
    margin = jnp.where((source_of == sequence[0]) | (taker == sequence[0]) | (sizes[taker] == 0), 0, jnp.maximum(margin, 0))
    passed = jax.random.randint(jax.random.fold_in(own, 4), (number_of // 2,), 0, 1 << 20) % (margin + 1)
    sizes = sizes.at[source_of].add(-passed).at[taker].add(passed)
    items = jnp.searchsorted(jnp.cumsum(sizes), jnp.arange(rows * top), side="right").astype(jnp.int32)
    grid = items.reshape(top, rows).T
    grid = grid[jax.random.permutation(jax.random.fold_in(own, 1), rows)]
    offset_by = jax.random.randint(jax.random.fold_in(own, 2), (rows, 1), 0, top)
    return jnp.take_along_axis(grid, (jnp.arange(top)[None, :] + offset_by) % top, axis=1)


def shares(number_of, total, limit, skew, full):
    loads = [(1 << 20) // math.isqrt(standing ** skew) + 1 for standing in range(1, number_of + 1)]
    largest = limit if full else min(limit, max(-(-total // number_of), total * loads[0] // sum(loads)))
    least = 1 if total - largest >= number_of - 1 else 0
    given, rest = [largest] + [least] * (number_of - 1), total - largest - least * (number_of - 1)
    while rest > 0:
        candidates = [i for i in range(1, number_of) if given[i] < largest] or [i for i in range(1, number_of) if given[i] < limit]
        pool, budget = sum([loads[i] for i in candidates]), rest
        for i in candidates:
            extra = min(limit - given[i], max(1, budget * loads[i] // pool), rest)
            given[i] = given[i] + extra
            rest = rest - extra
    return np.array(given)


def setup_inputs(seed: int = 0) -> dict:
    key_of = jax.random.split(jax.random.key(seed), 8)
    hidden = draw_hidden(jax.random.fold_in(key_of[7], 71), 0)
    output_weight = draw_output_weight(jax.random.fold_in(key_of[7], 71), 0)
    targets = plant(jax.random.randint(key_of[2], (TOKENS,), 0, V), jax.random.fold_in(key_of[2], 1), 0, V - 1).astype(jnp.int32)
    labels_keys = jax.random.split(jax.random.fold_in(key_of[3], 1), TOKENS // TOK_DEV)
    labels_turns = jax.random.permutation(jax.random.fold_in(key_of[3], 3), TOKENS // TOK_DEV)
    labels = jax.vmap(lambda own, number: shared_out(jax.random.fold_in(key_of[3], 2), own, number, TOK_DEV, K, 1, CAP, 2))(labels_keys, labels_turns).reshape((TOKENS, 1))
    prev_scores = draw_prev_scores(jax.random.fold_in(key_of[7], 71), 0)
    prev_probs = draw_prev_probs(jax.random.fold_in(key_of[7], 71), 0)
    next_domains = plant(jax.random.randint(key_of[6], (NEXT,), 0, K), jax.random.fold_in(key_of[6], 1), 0, K - 1).astype(jnp.int32)
    return dict(hidden=hidden, output_weight=output_weight, targets=targets, labels=labels, prev_scores=prev_scores, prev_probs=prev_probs, next_domains=next_domains)


def exploration_rates():
    earlier = min(1.0 / K, math.sqrt(math.log(K) / (K * (STEP - 1))))
    current = min(1.0 / K, math.sqrt(math.log(K) / (K * STEP)))
    return (earlier, current)

def reference(hidden, output_weight, targets, labels, prev_scores, prev_probs, next_domains):
    block_size = math.gcd(TOKENS, 256)

    def block_loss(pair):
        row_block, wanted = pair
        logits = jnp.dot(row_block, output_weight, preferred_element_type=jnp.float32)
        largest = lax.optimization_barrier(jnp.max(logits, axis=1))
        expsum = lax.optimization_barrier(jnp.sum(jnp.exp(logits - largest[:, None]), axis=1))
        picked = jnp.take_along_axis(logits, wanted[:, None], axis=1)[:, 0]
        return largest + jnp.log(expsum) - picked
    token_loss = lax.map(block_loss, (hidden.reshape(TOKENS // block_size, block_size, D), targets.reshape(TOKENS // block_size, block_size))).reshape(TOKENS)
    onehot = (labels[:, 0:1] == jnp.arange(K, dtype=jnp.int32)[None, :]).astype(jnp.float32)
    totals = jnp.dot(token_loss, onehot, precision=lax.Precision.HIGHEST)
    counts = lax.optimization_barrier(jnp.sum(onehot, axis=0))
    earlier, current = exploration_rates()
    new_scores = current / earlier * prev_scores + current * (totals / counts) / prev_probs
    largest_score = jnp.max(new_scores)
    weights = jnp.exp(new_scores - largest_score)
    probs = (1.0 - K * current) * (weights / jnp.sum(weights)) + current
    log_probs = jnp.log(probs)
    chosen = lax.optimization_barrier(jnp.sum(jnp.where(next_domains[:, None] == jnp.arange(K, dtype=jnp.int32)[None, :], probs[None, :], 0.0), axis=1))
    sample_weights = 1.0 / (K * chosen)
    return (token_loss, new_scores, log_probs, sample_weights)
```

```python
import functools
import math

import jax
import jax.numpy as jnp
from jax import lax
from jax.experimental import pallas as pl
from jax.experimental.pallas import tpu as pltpu
from jax.sharding import PartitionSpec as P

K = 64
STEP = 2000
LOW = -3.0e38
TILE = 512
NT = (((1,), (1,)), ((), ()))
AXES = ("dp", "tensor")


def exploration_rates():
    earlier = min(1.0 / K, math.sqrt(math.log(K) / (K * (STEP - 1))))
    current = min(1.0 / K, math.sqrt(math.log(K) / (K * STEP)))
    return (earlier, current)


def at_ring(place, count):
    return jnp.where(place < count // 2, 2 * place, 2 * (count - 1 - place) + 1)


def ring_place(index, count):
    return jnp.where(index % 2 == 0, index // 2, count - 1 - index // 2)


def column_of(table, index):
    lane = lax.broadcasted_iota(jnp.int32, table.shape, 1)
    return jnp.sum(jnp.where(lane == index, table, 0), axis=1, keepdims=True)


def slice_stats(rows, weight, wanted, vocab_offset, top, total, picked):
    count = rows.shape[0]
    vocab = weight.shape[0]
    top[...] = jnp.full_like(top, LOW)
    total[...] = jnp.zeros_like(total)
    picked[...] = jnp.zeros_like(picked)
    lane = lax.broadcasted_iota(jnp.int32, (count, 128), 1)
    wanted = jnp.broadcast_to(wanted, (count, 128)) - vocab_offset - lane
    for start in range(0, vocab, TILE):
        stop = min(start + TILE, vocab)
        logits = lax.dot_general(rows, weight[start:stop, :], NT, preferred_element_type=jnp.float32)
        fill = (start - stop) % 128
        if fill:
            logits = jnp.concatenate([logits, jnp.zeros((count, fill), jnp.float32)], axis=1)
        parts = [logits[:, i : i + 128] for i in range(0, logits.shape[1], 128)]
        chosen = picked[...]
        for i, part in enumerate(parts):
            chosen = chosen + jnp.where(wanted == start + 128 * i, part, 0.0)
        if fill:
            parts[-1] = jnp.where(lane < 128 - fill, parts[-1], LOW)
        picked[...] = chosen
        before = top[...]
        now = before
        for part in parts:
            now = jnp.maximum(now, part)
        added = total[...] * jnp.exp(before - now)
        for part in parts:
            added = added + jnp.exp(part - now)
        top[...] = now
        total[...] = added
    largest = jnp.max(top[...], axis=1, keepdims=True)
    summed = jnp.sum(total[...] * jnp.exp(top[...] - largest), axis=1, keepdims=True)
    pick = jnp.sum(picked[...], axis=1, keepdims=True)
    both = jnp.where(lane == 0, largest + jnp.log(summed), pick)
    if count % 128:
        both = jnp.concatenate([both, jnp.zeros((-count % 128, 128), jnp.float32)], axis=0)
    return jnp.transpose(both)[:8]


def first_kernel(place, rows, weight, wanted, out, held, top, total, picked, arrived):
    copy = pltpu.make_async_copy(weight, held, arrived)
    copy.start()
    copy.wait()
    out[...] = slice_stats(rows[...], held, wanted[...], place[0], top, total, picked)


def pair_kernel(step, place, one, two, held, table, out, top, total, picked):
    size = one.shape[0]
    core = place[1]
    if size == table.shape[0]:
        wanted = jnp.concatenate(
            [column_of(table[...], place[2 * step]), column_of(table[...], place[2 * step + 1])], axis=0
        )
    else:
        first = column_of(table[pl.ds(pl.multiple_of(core * size, 8), size), :], place[2 * step])
        second = column_of(table[pl.ds(pl.multiple_of((1 - core) * size, 8), size), :], place[2 * step])
        wanted = jnp.concatenate([first, second], axis=0)
    rows = jnp.concatenate([one[...], two[...]], axis=0)
    out[...] = slice_stats(rows, held, wanted, place[0], top, total, picked)


def pack_kernel(steps, halves, place, *refs):
    stats, out, table = refs[:-2], refs[-2], refs[-1]
    size = out.shape[3]
    for kind in range(2):
        table[kind, pl.ds(place[2], 1), :] = stats[0][kind : kind + 1, :size]
        for step in range(1, steps + 1):
            table[kind, pl.ds(place[2 * step + 2], 1), :] = stats[step][kind : kind + 1, :size]
            table[kind, pl.ds(place[2 * step + 3], 1), :] = stats[step][kind : kind + 1, size : 2 * size]
        if halves:
            last = stats[steps + 1][kind : kind + 1, :size]
            one, two = last[:, : size // 2], last[:, size // 2 :]
            swapped = jnp.concatenate([two, one], axis=1)
            table[kind, pl.ds(place[2 * steps + 4], 1), :] = jnp.where(place[1] == 0, last, swapped)
    out[...] = jnp.broadcast_to(table[...][None], out.shape)


def row_of(column):
    size = column.shape[0]
    same = lax.broadcasted_iota(jnp.int32, (size, size), 0) == lax.broadcasted_iota(jnp.int32, (size, size), 1)
    return jnp.sum(jnp.where(same, column, 0.0), axis=0, keepdims=True)


def last_kernel(place, stats, labels, scores, probs_before, domains, loss_out, score_out, log_out, weight_out, kept, kept_scores):
    dp_index, tensor_index = place[0], place[1]
    groups, size = kept.shape
    share = loss_out.shape[1]
    owned = score_out.shape[1]
    lse = stats[:, 0]
    overall = jnp.max(lse, axis=0)
    loss = overall + jnp.log(jnp.sum(jnp.exp(lse - overall[None]), axis=0)) - jnp.sum(stats[:, 1], axis=0)
    kept[...] = loss
    own = kept[pl.ds(dp_index, 1), :]
    picked = own[:, :share]
    for i in range(1, size // share):
        picked = jnp.where(tensor_index == i, own[:, i * share : (i + 1) * share], picked)
    loss_out[...] = picked
    number = lax.broadcasted_iota(jnp.int32, (K, size), 0)
    sums = jnp.zeros((K, size), jnp.float32)
    counts = jnp.zeros((K, size), jnp.float32)
    for i in range(groups):
        match = number == labels[i : i + 1, :]
        sums = sums + jnp.where(match, loss[i : i + 1, :], 0.0)
        counts = counts + jnp.where(match, 1.0, 0.0)
    sums = jnp.sum(sums, axis=1, keepdims=True)
    counts = jnp.sum(counts, axis=1, keepdims=True)
    earlier, current = exploration_rates()
    new = current / earlier * scores[...] + current * (sums / counts) / probs_before[...]
    kept_scores[...] = jnp.broadcast_to(new, kept_scores.shape)
    score_out[...] = row_of(kept_scores[pl.ds(pl.multiple_of(dp_index * owned, owned), owned), :][:, :1])
    weights = jnp.exp(new - jnp.max(new, axis=0, keepdims=True))
    probs = (1.0 - K * current) * (weights / jnp.sum(weights, axis=0, keepdims=True)) + current
    log_out[...] = row_of(jnp.log(probs))
    known = lax.broadcasted_iota(jnp.int32, (K, domains.shape[1]), 0) == domains[...]
    weight_out[...] = 1.0 / (K * jnp.sum(jnp.where(known, probs, 0.0), axis=0, keepdims=True))


def body(hidden, output_weight, targets, labels, prev_scores, prev_probs, next_domains):
    size, width = hidden.shape
    vocab = output_weight.shape[1]
    dp_count = lax.axis_size("dp")
    tensor_count = lax.axis_size("tensor")
    dp_index = lax.axis_index("dp")
    tensor_index = lax.axis_index("tensor")
    core = tensor_index % 2
    place = ring_place(dp_index, dp_count)
    steps = dp_count // 2 - 1
    up = 1 - 2 * core
    places = [lax.axis_index(AXES) * vocab, core]
    numbers = [dp_index, dp_index]
    for step in range(1, steps + 2):
        numbers += [
            at_ring((place - up * step + dp_count) % dp_count, dp_count),
            at_ring((place + up * step + dp_count) % dp_count, dp_count),
        ]
    places = jnp.stack(places + numbers).astype(jnp.int32)
    order = [2 * i for i in range(dp_count // 2)] + [2 * i + 1 for i in reversed(range(dp_count // 2))]
    along = []
    for p in range(dp_count):
        for t in range(tensor_count):
            to = order[(p + 1 - 2 * (t % 2)) % dp_count]
            along.append((order[p] * tensor_count + t, to * tensor_count + t))
    across = [(t, t ^ 1) for t in range(tensor_count)]

    smem = pl.BlockSpec(memory_space=pltpu.SMEM)
    vmem = pl.BlockSpec(memory_space=pltpu.VMEM)
    whole = pl.BlockSpec(memory_space=pl.ANY)
    fixed = lambda x: pltpu.with_memory_space_constraint(x, pltpu.VMEM)

    def scratch(rows):
        return [pltpu.VMEM((rows, 128), jnp.float32)] * 3

    def cost(rows):
        return pl.CostEstimate(
            flops=2 * rows * width * vocab, bytes_accessed=2 * (rows * width), transcendentals=rows * vocab
        )

    limit = pltpu.CompilerParams(vmem_limit_bytes=12 << 20)
    padded = -(-size // 128) * 128

    stats, held = pl.pallas_call(
        first_kernel,
        in_specs=[smem, vmem, whole, vmem],
        out_specs=[vmem, vmem],
        out_shape=[
            jax.ShapeDtypeStruct((8, padded), jnp.float32),
            pltpu.VMEM((vocab, width), jnp.bfloat16),
        ],
        scratch_shapes=scratch(size) + [pltpu.SemaphoreType.DMA],
        compiler_params=limit,
        cost_estimate=cost(2 * size),
    )(places, hidden, output_weight.T, targets[:, None])
    gathered = [stats]

    packed = jnp.concatenate([labels[:, 0].astype(jnp.float32), targets.astype(jnp.float32), prev_scores, prev_probs])
    sent = jnp.broadcast_to(packed[None], (dp_count, packed.shape[0]))
    info = lax.all_to_all(sent, "dp", split_axis=0, concat_axis=0, tiled=True)
    every_label = info[:, :size].astype(jnp.int32)
    table = info[:, size : 2 * size].astype(jnp.int32).T
    owned = prev_scores.shape[0]
    every_score = info[:, 2 * size : 2 * size + owned].reshape(K, 1)
    every_prob = info[:, 2 * size + owned :].reshape(K, 1)

    def pair(step, one, two):
        rows = 2 * one.shape[0]
        return pl.pallas_call(
            functools.partial(pair_kernel, step + 1),
            in_specs=[smem, vmem, vmem, vmem, vmem],
            out_specs=vmem,
            out_shape=jax.ShapeDtypeStruct((8, -(-rows // 128) * 128), jnp.float32),
            scratch_shapes=scratch(rows),
            compiler_params=limit,
            cost_estimate=cost(rows),
        )(places, fixed(one), fixed(two), fixed(held), table)

    block = hidden
    for step in range(1, steps + 1):
        block = lax.ppermute(block, AXES, along)
        other = lax.ppermute(block, "tensor", across)
        gathered.append(pair(step, block, other))
    half = lax.dynamic_slice_in_dim(block, core * (size // 2), size // 2, 0)
    half = lax.ppermute(half, AXES, along)
    other = lax.ppermute(half, "tensor", across)
    gathered.append(pair(steps + 1, half, other))

    devices = dp_count * tensor_count
    mine = pl.pallas_call(
        functools.partial(pack_kernel, steps, True),
        in_specs=[smem] + [vmem] * len(gathered),
        out_specs=vmem,
        out_shape=jax.ShapeDtypeStruct((devices, 2, dp_count, size), jnp.float32),
        scratch_shapes=[pltpu.VMEM((2, dp_count, size), jnp.float32)],
        compiler_params=limit,
    )(places, *gathered)
    every = lax.all_to_all(mine, AXES, split_axis=0, concat_axis=0, tiled=True)

    loss, scores, logs, weights = pl.pallas_call(
        last_kernel,
        in_specs=[smem] + [vmem] * 5,
        out_specs=[vmem] * 4,
        out_shape=[
            jax.ShapeDtypeStruct((1, size // tensor_count), jnp.float32),
            jax.ShapeDtypeStruct((1, owned), jnp.float32),
            jax.ShapeDtypeStruct((1, K), jnp.float32),
            jax.ShapeDtypeStruct((1, next_domains.shape[0]), jnp.float32),
        ],
        scratch_shapes=[pltpu.VMEM((dp_count, size), jnp.float32), pltpu.VMEM((K, 128), jnp.float32)],
        compiler_params=limit,
    )(
        jnp.stack([dp_index, tensor_index]).astype(jnp.int32),
        every,
        every_label,
        every_score,
        every_prob,
        next_domains[None, :],
    )
    return (loss[0], scores[0], logs[0], weights[0])


def solution(mesh):
    placed = (
        P("dp", None),
        P(None, AXES),
        P("dp"),
        P("dp", None),
        P("dp"),
        P("dp"),
        P("dp"),
    )
    return jax.shard_map(
        body,
        mesh=mesh,
        in_specs=placed,
        out_specs=(P(AXES), P("dp"), P(), P("dp")),
        check_vma=False,
    )
```

```python
import functools
import math

import jax
import jax.numpy as jnp
from jax import lax
from jax.experimental import pallas as pl
from jax.experimental.pallas import tpu as pltpu
from jax.sharding import PartitionSpec as P

K = 64
STEP = 2000
LOW = -3.0e38
TILE = 512
NT = (((1,), (1,)), ((), ()))
AXES = ("dp", "tensor")


def exploration_rates():
    earlier = min(1.0 / K, math.sqrt(math.log(K) / (K * (STEP - 1))))
    current = min(1.0 / K, math.sqrt(math.log(K) / (K * STEP)))
    return (earlier, current)


def at_ring(place, count):
    place = lax.rem(place + count, count)
    return jnp.where(place < count // 2, 2 * place, 2 * (count - 1 - place) + 1)


def ring_place(index, count):
    half = lax.div(index, 2)
    return jnp.where(lax.rem(index, 2) == 0, half, count - 1 - half)


def slice_stats(rows, ending, weight, wanted, vocab_offset, held, arrived, top, total, picked):
    count = rows.shape[0]
    vocab = weight.shape[0]
    full = (vocab - 1) // TILE
    copies = [
        pltpu.make_async_copy(weight.at[pl.ds(i * TILE, TILE), :], held.at[pl.ds(i * TILE, TILE), :], arrived.at[i])
        for i in range(full)
    ]
    for copy in copies:
        copy.start()
    top[...] = jnp.full_like(top, LOW)
    total[...] = jnp.zeros_like(total)
    picked[...] = jnp.zeros_like(picked)
    lane = lax.broadcasted_iota(jnp.int32, (count, 128), 1)
    wanted = jnp.broadcast_to(wanted, (count, 128)) - vocab_offset - lane
    for tile in [full] + list(range(full)):
        start = tile * TILE
        if tile < full:
            copies[tile].wait()
            columns = held[start : start + TILE, :]
        else:
            columns = ending[...]
        logits = lax.dot_general(rows, columns, NT, preferred_element_type=jnp.float32)
        parts = []
        chosen = picked[...]
        for i in range(start, min(start + TILE, vocab), 128):
            part = logits[:, i - start : i - start + 128]
            if i + 128 > vocab:
                part = jnp.where(lane < vocab - i, part, LOW)
                chosen = chosen + jnp.where((wanted == i) & (lane < vocab - i), part, 0.0)
            else:
                chosen = chosen + jnp.where(wanted == i, part, 0.0)
            parts.append(part)
        picked[...] = chosen
        before = top[...]
        now = before
        for part in parts:
            now = jnp.maximum(now, part)
        added = total[...] * jnp.exp(before - now)
        for part in parts:
            added = added + jnp.exp(part - now)
        top[...] = now
        total[...] = added
    largest = jnp.max(top[...], axis=1, keepdims=True)
    summed = jnp.sum(total[...] * jnp.exp(top[...] - largest), axis=1, keepdims=True)
    pick = jnp.sum(picked[...], axis=1, keepdims=True)
    both = jnp.where(lane == 0, largest + jnp.log(summed), pick)
    if count % 128:
        both = jnp.concatenate([both, jnp.zeros((-count % 128, 128), jnp.float32)], axis=0)
    return jnp.transpose(both)[:8]


def join_kernel(hidden, target, out):
    width = hidden.shape[1]
    lane = lax.broadcasted_iota(jnp.int32, (hidden.shape[0], out.shape[1] - width), 1)
    wanted = target[...]
    digits = jnp.where(lane == 0, wanted & 255, jnp.where(lane == 1, (wanted >> 8) & 255, wanted >> 16))
    out[:, :width] = hidden[...]
    out[:, width:] = jnp.where(lane < 3, digits, 0).astype(jnp.float32).astype(out.dtype)


def targets_of(rows, width):
    digits = rows[:, width:].astype(jnp.float32)
    lane = lax.broadcasted_iota(jnp.int32, digits.shape, 1)
    scale = jnp.where(lane == 0, 1.0, jnp.where(lane == 1, 256.0, 65536.0))
    return jnp.sum(digits * scale, axis=1, keepdims=True).astype(jnp.int32)


def offset_of(place, tensor_count, vocab):
    return (place[0] * tensor_count + place[1]) * vocab


def first_kernel(tensor_count, place, rows, ending, weight, out, *scratch):
    vocab, width = weight.shape
    wanted = targets_of(rows, width)
    offset = offset_of(place, tensor_count, vocab)
    out[...] = slice_stats(rows[:, :width], ending, weight, wanted, offset, *scratch)


def pair_kernel(tensor_count, place, one, two, ending, weight, out, *scratch):
    vocab, width = weight.shape
    wanted = jnp.concatenate([targets_of(one, width), targets_of(two, width)], axis=0)
    rows = jnp.concatenate([one[:, :width], two[:, :width]], axis=0)
    offset = offset_of(place, tensor_count, vocab)
    out[...] = slice_stats(rows, ending, weight, wanted, offset, *scratch)


def half_kernel(place, block, out):
    size = out.shape[0]
    start = pl.multiple_of(lax.rem(place[1], 2) * size, size)
    out[...] = block[pl.ds(start, size), :]


def pack_kernel(size, place, labels, scores, probs, *refs):
    stats, out, table = refs[:-2], refs[-2], refs[-1]
    steps = len(stats) - 2
    count = table.shape[1]
    core = lax.rem(place[1], 2)
    own = ring_place(place[0], count)
    up = 1 - 2 * core
    table[...] = jnp.zeros_like(table)
    for kind in range(2):

        def put(index, row):
            table[kind, pl.ds(index, 1), :size] = row

        put(place[0], stats[0][kind : kind + 1, :size])
        for step in range(1, steps + 1):
            put(at_ring(own - up * step, count), stats[step][kind : kind + 1, :size])
            put(at_ring(own + up * step, count), stats[step][kind : kind + 1, size : 2 * size])
        last = stats[-1][kind : kind + 1, :size]
        swapped = jnp.concatenate([last[:, size // 2 :], last[:, : size // 2]], axis=1)
        put(at_ring(own + steps + 1, count), jnp.where(core == 0, last, swapped))
    rest = table.shape[2] - size
    for i in range(size // rest):
        table[0, i : i + 1, size:] = labels[:, i * rest : (i + 1) * rest].astype(jnp.float32)
    owned = scores.shape[1]
    table[1, 0:1, size : size + owned] = scores[...]
    table[1, 1:2, size : size + owned] = probs[...]
    out[...] = jnp.broadcast_to(table[...][None], out.shape)


def row_of(column):
    size = column.shape[0]
    same = lax.broadcasted_iota(jnp.int32, (size, size), 0) == lax.broadcasted_iota(jnp.int32, (size, size), 1)
    return jnp.sum(jnp.where(same, column, 0.0), axis=0, keepdims=True)


def last_kernel(tensor_count, place, stats, domains, loss_out, score_out, log_out, weight_out, kept, kept_scores):
    dp_index, tensor_index = place[0], place[1]
    groups, size = kept.shape
    share = loss_out.shape[1]
    owned = score_out.shape[1]
    rest = stats.shape[3] - size
    lse = stats[:, 0, :, :size]
    overall = jnp.max(lse, axis=0)
    loss = overall + jnp.log(jnp.sum(jnp.exp(lse - overall[None]), axis=0)) - jnp.sum(stats[:, 1, :, :size], axis=0)
    kept[...] = loss
    own = kept[pl.ds(dp_index, 1), :]
    picked = own[:, :share]
    for i in range(1, tensor_count):
        picked = jnp.where(tensor_index == i, own[:, i * share : (i + 1) * share], picked)
    loss_out[...] = picked
    number = lax.broadcasted_iota(jnp.int32, (K, size), 0).astype(jnp.float32)
    place_of = lax.broadcasted_iota(jnp.int32, (K, owned), 0) - lax.broadcasted_iota(jnp.int32, (K, owned), 1)
    sums = jnp.zeros((K, size), jnp.float32)
    counts = jnp.zeros((K, size), jnp.float32)
    scores = jnp.zeros((K, owned), jnp.float32)
    before = jnp.zeros((K, owned), jnp.float32)
    for i in range(groups):
        source = i * tensor_count
        label = jnp.concatenate([stats[source, 0, j : j + 1, size:] for j in range(size // rest)], axis=1)
        match = number == label
        sums = sums + jnp.where(match, loss[i : i + 1, :], 0.0)
        counts = counts + jnp.where(match, 1.0, 0.0)
        here = place_of == i * owned
        scores = scores + jnp.where(here, stats[source, 1, 0:1, size : size + owned], 0.0)
        before = before + jnp.where(here, stats[source, 1, 1:2, size : size + owned], 0.0)
    sums = jnp.sum(sums, axis=1, keepdims=True)
    counts = jnp.sum(counts, axis=1, keepdims=True)
    scores = jnp.sum(scores, axis=1, keepdims=True)
    before = jnp.sum(before, axis=1, keepdims=True)
    earlier, current = exploration_rates()
    new = current / earlier * scores + current * (sums / counts) / before
    kept_scores[...] = jnp.broadcast_to(new, kept_scores.shape)
    score_out[...] = row_of(kept_scores[pl.ds(pl.multiple_of(dp_index * owned, owned), owned), :][:, :1])
    weights = jnp.exp(new - jnp.max(new, axis=0, keepdims=True))
    probs = (1.0 - K * current) * (weights / jnp.sum(weights, axis=0, keepdims=True)) + current
    log_out[...] = row_of(jnp.log(probs))
    known = lax.broadcasted_iota(jnp.int32, (K, domains.shape[1]), 0) == domains[...]
    weight_out[...] = 1.0 / (K * jnp.sum(jnp.where(known, probs, 0.0), axis=0, keepdims=True))


def body(hidden, output_weight, targets, labels, prev_scores, prev_probs, next_domains):
    size, width = hidden.shape
    vocab = output_weight.shape[1]
    dp_count = lax.axis_size("dp")
    tensor_count = lax.axis_size("tensor")
    devices = dp_count * tensor_count
    owned = prev_scores.shape[0]
    steps = dp_count // 2 - 1
    place = jnp.stack([lax.axis_index("dp"), lax.axis_index("tensor")]).astype(jnp.int32)
    order = [2 * i for i in range(dp_count // 2)] + [2 * i + 1 for i in reversed(range(dp_count // 2))]
    along = []
    for p in range(dp_count):
        for t in range(tensor_count):
            to = order[(p + 1 - 2 * (t % 2)) % dp_count]
            along.append((order[p] * tensor_count + t, to * tensor_count + t))
    across = [(t, t ^ 1) for t in range(tensor_count)]

    smem = pl.BlockSpec(memory_space=pltpu.SMEM)
    vmem = pl.BlockSpec(memory_space=pltpu.VMEM)
    whole = pl.BlockSpec(memory_space=pl.ANY)
    fixed = lambda x: pltpu.with_memory_space_constraint(x, pltpu.VMEM)
    limit = pltpu.CompilerParams(vmem_limit_bytes=12 << 20)

    def up_to(count, unit):
        return -(-count // unit) * unit

    full = (vocab - 1) // TILE
    weight = output_weight.T

    def stats_of(*blocks):
        rows = sum(block.shape[0] for block in blocks)
        return pl.pallas_call(
            functools.partial(first_kernel if len(blocks) == 1 else pair_kernel, tensor_count),
            grid=(1,),
            in_specs=[smem] + [vmem] * len(blocks) + [pl.BlockSpec((TILE, width), lambda i: (full, 0)), whole],
            out_specs=vmem,
            out_shape=jax.ShapeDtypeStruct((8, up_to(rows, 128)), jnp.float32),
            scratch_shapes=[pltpu.VMEM((max(full, 1) * TILE, width), weight.dtype), pltpu.SemaphoreType.DMA((max(full, 1),))]
            + [pltpu.VMEM((rows, 128), jnp.float32)] * 3,
            compiler_params=pltpu.CompilerParams(vmem_limit_bytes=44 << 20),
            cost_estimate=pl.CostEstimate(
                flops=2 * rows * width * vocab, bytes_accessed=2 * width * vocab, transcendentals=rows * vocab
            ),
        )(place, *[fixed(block) for block in blocks], weight, weight)

    block = pl.pallas_call(
        join_kernel,
        in_specs=[vmem, vmem],
        out_specs=vmem,
        out_shape=pltpu.VMEM((size, width + 128), hidden.dtype),
        compiler_params=limit,
    )(hidden, targets[:, None])

    def half(block):
        return pl.pallas_call(
            half_kernel,
            in_specs=[smem, vmem],
            out_specs=vmem,
            out_shape=pltpu.VMEM((block.shape[0] // 2, block.shape[1]), block.dtype),
            compiler_params=limit,
        )(place, fixed(block))

    coming = lax.ppermute(block, AXES, along)
    gathered = [stats_of(block)]
    for step in range(1, steps + 2):
        block, gathered[-1] = lax.optimization_barrier((coming, gathered[-1]))
        other = lax.ppermute(block, "tensor", across)
        if step <= steps:
            coming = lax.ppermute(block if step < steps else half(block), AXES, along)
        gathered.append(stats_of(block, other))

    mine = pl.pallas_call(
        functools.partial(pack_kernel, size),
        in_specs=[smem] + [vmem] * (len(gathered) + 3),
        out_specs=vmem,
        out_shape=jax.ShapeDtypeStruct((devices, 2, dp_count, up_to(size, 128)), jnp.float32),
        scratch_shapes=[pltpu.VMEM((2, dp_count, up_to(size, 128)), jnp.float32)],
        compiler_params=limit,
    )(place, labels.reshape(1, size), prev_scores[None, :], prev_probs[None, :], *gathered)
    every = lax.all_to_all(mine, AXES, split_axis=0, concat_axis=0, tiled=True)

    loss, scores, logs, weights = pl.pallas_call(
        functools.partial(last_kernel, tensor_count),
        in_specs=[smem, vmem, vmem],
        out_specs=[vmem] * 4,
        out_shape=[
            jax.ShapeDtypeStruct((1, size // tensor_count), jnp.float32),
            jax.ShapeDtypeStruct((1, owned), jnp.float32),
            jax.ShapeDtypeStruct((1, K), jnp.float32),
            jax.ShapeDtypeStruct((1, next_domains.shape[0]), jnp.float32),
        ],
        scratch_shapes=[pltpu.VMEM((dp_count, size), jnp.float32), pltpu.VMEM((K, 128), jnp.float32)],
        compiler_params=pltpu.CompilerParams(vmem_limit_bytes=24 << 20),
    )(place, every, next_domains[None, :])
    return (loss[0], scores[0], logs[0], weights[0])


def solution(mesh):
    placed = (
        P("dp", None),
        P(None, AXES),
        P("dp"),
        P("dp", None),
        P("dp"),
        P("dp"),
        P("dp"),
    )
    return jax.shard_map(
        body,
        mesh=mesh,
        in_specs=placed,
        out_specs=(P(AXES), P("dp"), P(), P("dp")),
        check_vma=False,
    )
```

```python
import functools
import math

import jax
import jax.numpy as jnp
from jax import lax
from jax.experimental import pallas as pl
from jax.experimental.pallas import tpu as pltpu
from jax.sharding import PartitionSpec as P

K = 64
STEP = 2000
LOW = -3.0e38
TILE = 512
KEEP = 7
NT = (((1,), (1,)), ((), ()))
AXES = ("dp", "tensor")


def exploration_rates():
    earlier = min(1.0 / K, math.sqrt(math.log(K) / (K * (STEP - 1))))
    current = min(1.0 / K, math.sqrt(math.log(K) / (K * STEP)))
    return (earlier, current)


def at_ring(place, count):
    place = lax.rem(place + count, count)
    return jnp.where(place < count // 2, 2 * place, 2 * (count - 1 - place) + 1)


def ring_place(index, count):
    half = lax.div(index, 2)
    return jnp.where(lax.rem(index, 2) == 0, half, count - 1 - half)


def slice_stats(rows, tiles, copies, vocab, wanted, vocab_offset, top, total, picked):
    count = rows.shape[0]
    full = len(tiles) - 1
    top[...] = jnp.full_like(top, LOW)
    total[...] = jnp.zeros_like(total)
    picked[...] = jnp.zeros_like(picked)
    lane = lax.broadcasted_iota(jnp.int32, (count, 128), 1)
    wanted = jnp.broadcast_to(wanted, (count, 128)) - vocab_offset - lane
    for tile in [full] + list(range(full)):
        start = tile * TILE
        if tile in copies:
            copies[tile].wait()
        logits = lax.dot_general(rows, tiles[tile][...], NT, preferred_element_type=jnp.float32)
        parts = []
        chosen = picked[...]
        for i in range(start, min(start + TILE, vocab), 128):
            part = logits[:, i - start : i - start + 128]
            if i + 128 > vocab:
                part = jnp.where(lane < vocab - i, part, LOW)
                chosen = chosen + jnp.where((wanted == i) & (lane < vocab - i), part, 0.0)
            else:
                chosen = chosen + jnp.where(wanted == i, part, 0.0)
            parts.append(part)
        picked[...] = chosen
        before = top[...]
        now = before
        for part in parts:
            now = jnp.maximum(now, part)
        added = total[...] * jnp.exp(before - now)
        for part in parts:
            added = added + jnp.exp(part - now)
        top[...] = now
        total[...] = added
    largest = jnp.max(top[...], axis=1, keepdims=True)
    summed = jnp.sum(total[...] * jnp.exp(top[...] - largest), axis=1, keepdims=True)
    pick = jnp.sum(picked[...], axis=1, keepdims=True)
    both = jnp.where(lane == 0, largest + jnp.log(summed), pick)
    if count % 128:
        both = jnp.concatenate([both, jnp.zeros((-count % 128, 128), jnp.float32)], axis=0)
    return jnp.transpose(both)[:8]


def join_kernel(hidden, target, out):
    width = hidden.shape[1]
    lane = lax.broadcasted_iota(jnp.int32, (hidden.shape[0], out.shape[1] - width), 1)
    wanted = target[...]
    digits = jnp.where(lane == 0, wanted & 255, jnp.where(lane == 1, (wanted >> 8) & 255, wanted >> 16))
    out[:, :width] = hidden[...]
    out[:, width:] = jnp.where(lane < 3, digits, 0).astype(jnp.float32).astype(out.dtype)


def targets_of(rows, width):
    digits = rows[:, width:].astype(jnp.float32)
    lane = lax.broadcasted_iota(jnp.int32, digits.shape, 1)
    scale = jnp.where(lane == 0, 1.0, jnp.where(lane == 1, 256.0, 65536.0))
    return jnp.sum(digits * scale, axis=1, keepdims=True).astype(jnp.int32)


def offset_of(place, tensor_count, vocab):
    return (place[0] * tensor_count + place[1]) * vocab


def start_copies(weight, tiles, arrived, first):
    copies = {}
    for i in range(first, first + len(tiles)):
        copies[i] = pltpu.make_async_copy(weight.at[pl.ds(i * TILE, TILE), :], tiles[i - first], arrived.at[i - first])
        copies[i].start()
    return copies


def first_kernel(tensor_count, keep, place, rows, ending, weight, out, *rest):
    vocab, width = weight.shape
    full = (vocab - 1) // TILE
    kept, rest = rest[: keep + 1], rest[keep + 1 :]
    streamed, rest = rest[: full - keep], rest[full - keep :]
    tiles = list(kept[:keep]) + list(streamed)
    copies = start_copies(weight, tiles, rest[0], 0)
    kept[keep][...] = ending[...]
    wanted = targets_of(rows, width)
    offset = offset_of(place, tensor_count, vocab)
    out[...] = slice_stats(rows[:, :width], tiles + [ending], copies, vocab, wanted, offset, *rest[1:])


def pair_kernel(tensor_count, keep, place, one, two, weight, *rest):
    vocab, width = weight.shape
    full = (vocab - 1) // TILE
    kept, out, rest = rest[: keep + 1], rest[keep + 1], rest[keep + 2 :]
    streamed, rest = rest[: full - keep], rest[full - keep :]
    tiles = list(kept[:keep]) + list(streamed)
    copies = start_copies(weight, streamed, rest[0], keep)
    wanted = jnp.concatenate([targets_of(one, width), targets_of(two, width)], axis=0)
    rows = jnp.concatenate([one[:, :width], two[:, :width]], axis=0)
    offset = offset_of(place, tensor_count, vocab)
    out[...] = slice_stats(rows, tiles + [kept[keep]], copies, vocab, wanted, offset, *rest[1:])


def half_kernel(place, block, out):
    size = out.shape[0]
    start = pl.multiple_of(lax.rem(place[1], 2) * size, size)
    out[...] = block[pl.ds(start, size), :]


def pack_kernel(size, place, labels, scores, probs, *refs):
    stats, out, table = refs[:-2], refs[-2], refs[-1]
    steps = len(stats) - 2
    count = table.shape[1]
    core = lax.rem(place[1], 2)
    own = ring_place(place[0], count)
    up = 1 - 2 * core
    table[...] = jnp.zeros_like(table)
    for kind in range(2):

        def put(index, row):
            table[kind, pl.ds(index, 1), :size] = row

        put(place[0], stats[0][kind : kind + 1, :size])
        for step in range(1, steps + 1):
            put(at_ring(own - up * step, count), stats[step][kind : kind + 1, :size])
            put(at_ring(own + up * step, count), stats[step][kind : kind + 1, size : 2 * size])
        last = stats[-1][kind : kind + 1, :size]
        swapped = jnp.concatenate([last[:, size // 2 :], last[:, : size // 2]], axis=1)
        put(at_ring(own + steps + 1, count), jnp.where(core == 0, last, swapped))
    rest = table.shape[2] - size
    for i in range(size // rest):
        table[0, i : i + 1, size:] = labels[:, i * rest : (i + 1) * rest].astype(jnp.float32)
    owned = scores.shape[1]
    table[1, 0:1, size : size + owned] = scores[...]
    table[1, 1:2, size : size + owned] = probs[...]
    out[...] = jnp.broadcast_to(table[...][None], out.shape)


def row_of(column):
    size = column.shape[0]
    same = lax.broadcasted_iota(jnp.int32, (size, size), 0) == lax.broadcasted_iota(jnp.int32, (size, size), 1)
    return jnp.sum(jnp.where(same, column, 0.0), axis=0, keepdims=True)


def last_kernel(tensor_count, place, stats, domains, loss_out, score_out, log_out, weight_out, kept, kept_scores):
    dp_index, tensor_index = place[0], place[1]
    groups, size = kept.shape
    share = loss_out.shape[1]
    owned = score_out.shape[1]
    rest = stats.shape[3] - size
    lse = stats[:, 0, :, :size]
    overall = jnp.max(lse, axis=0)
    loss = overall + jnp.log(jnp.sum(jnp.exp(lse - overall[None]), axis=0)) - jnp.sum(stats[:, 1, :, :size], axis=0)
    kept[...] = loss
    own = kept[pl.ds(dp_index, 1), :]
    picked = own[:, :share]
    for i in range(1, tensor_count):
        picked = jnp.where(tensor_index == i, own[:, i * share : (i + 1) * share], picked)
    loss_out[...] = picked
    number = lax.broadcasted_iota(jnp.int32, (K, size), 0).astype(jnp.float32)
    place_of = lax.broadcasted_iota(jnp.int32, (K, owned), 0) - lax.broadcasted_iota(jnp.int32, (K, owned), 1)
    sums = jnp.zeros((K, size), jnp.float32)
    counts = jnp.zeros((K, size), jnp.float32)
    scores = jnp.zeros((K, owned), jnp.float32)
    before = jnp.zeros((K, owned), jnp.float32)
    for i in range(groups):
        source = i * tensor_count
        label = jnp.concatenate([stats[source, 0, j : j + 1, size:] for j in range(size // rest)], axis=1)
        match = number == label
        sums = sums + jnp.where(match, loss[i : i + 1, :], 0.0)
        counts = counts + jnp.where(match, 1.0, 0.0)
        here = place_of == i * owned
        scores = scores + jnp.where(here, stats[source, 1, 0:1, size : size + owned], 0.0)
        before = before + jnp.where(here, stats[source, 1, 1:2, size : size + owned], 0.0)
    sums = jnp.sum(sums, axis=1, keepdims=True)
    counts = jnp.sum(counts, axis=1, keepdims=True)
    scores = jnp.sum(scores, axis=1, keepdims=True)
    before = jnp.sum(before, axis=1, keepdims=True)
    earlier, current = exploration_rates()
    new = current / earlier * scores + current * (sums / counts) / before
    kept_scores[...] = jnp.broadcast_to(new, kept_scores.shape)
    score_out[...] = row_of(kept_scores[pl.ds(pl.multiple_of(dp_index * owned, owned), owned), :][:, :1])
    weights = jnp.exp(new - jnp.max(new, axis=0, keepdims=True))
    probs = (1.0 - K * current) * (weights / jnp.sum(weights, axis=0, keepdims=True)) + current
    log_out[...] = row_of(jnp.log(probs))
    known = lax.broadcasted_iota(jnp.int32, (K, domains.shape[1]), 0) == domains[...]
    weight_out[...] = 1.0 / (K * jnp.sum(jnp.where(known, probs, 0.0), axis=0, keepdims=True))


def body(hidden, output_weight, targets, labels, prev_scores, prev_probs, next_domains):
    size, width = hidden.shape
    vocab = output_weight.shape[1]
    dp_count = lax.axis_size("dp")
    tensor_count = lax.axis_size("tensor")
    devices = dp_count * tensor_count
    owned = prev_scores.shape[0]
    steps = dp_count // 2 - 1
    place = jnp.stack([lax.axis_index("dp"), lax.axis_index("tensor")]).astype(jnp.int32)
    order = [2 * i for i in range(dp_count // 2)] + [2 * i + 1 for i in reversed(range(dp_count // 2))]
    along = []
    for p in range(dp_count):
        for t in range(tensor_count):
            to = order[(p + 1 - 2 * (t % 2)) % dp_count]
            along.append((order[p] * tensor_count + t, to * tensor_count + t))
    across = [(t, t ^ 1) for t in range(tensor_count)]

    smem = pl.BlockSpec(memory_space=pltpu.SMEM)
    vmem = pl.BlockSpec(memory_space=pltpu.VMEM)
    whole = pl.BlockSpec(memory_space=pl.ANY)
    fixed = lambda x: pltpu.with_memory_space_constraint(x, pltpu.VMEM)
    limit = pltpu.CompilerParams(vmem_limit_bytes=12 << 20)

    def up_to(count, unit):
        return -(-count // unit) * unit

    full = (vocab - 1) // TILE
    keep = min(KEEP, full)
    weight = output_weight.T
    tile = pltpu.VMEM((TILE, width), weight.dtype)

    def stats_of(blocks, kept):
        rows = sum(block.shape[0] for block in blocks)
        first = not kept
        table = jax.ShapeDtypeStruct((8, up_to(rows, 128)), jnp.float32)
        return pl.pallas_call(
            functools.partial(first_kernel if first else pair_kernel, tensor_count, keep),
            grid=(1,),
            in_specs=[smem]
            + [vmem] * len(blocks)
            + ([pl.BlockSpec((TILE, width), lambda i: (full, 0))] if first else [])
            + [whole]
            + [vmem] * len(kept),
            out_specs=[vmem] * (keep + 2) if first else vmem,
            out_shape=[table] + [tile] * (keep + 1) if first else table,
            scratch_shapes=[tile] * (full - keep)
            + [pltpu.SemaphoreType.DMA((full if first else max(full - keep, 1),))]
            + [pltpu.VMEM((rows, 128), jnp.float32)] * 3,
            compiler_params=pltpu.CompilerParams(vmem_limit_bytes=(10 + 4 * (full - keep) << 20)),
            cost_estimate=pl.CostEstimate(
                flops=2 * rows * width * vocab, bytes_accessed=2 * width * vocab, transcendentals=rows * vocab
            ),
        )(place, *[fixed(x) for x in blocks], *([weight] if first else []), weight, *[fixed(x) for x in kept])

    block = pl.pallas_call(
        join_kernel,
        in_specs=[vmem, vmem],
        out_specs=vmem,
        out_shape=pltpu.VMEM((size, width + 128), hidden.dtype),
        compiler_params=limit,
    )(hidden, targets[:, None])

    def half(block):
        return pl.pallas_call(
            half_kernel,
            in_specs=[smem, vmem],
            out_specs=vmem,
            out_shape=pltpu.VMEM((block.shape[0] // 2, block.shape[1]), block.dtype),
            compiler_params=limit,
        )(place, fixed(block))

    coming = lax.ppermute(block, AXES, along)
    stats, *kept = stats_of([block], [])
    gathered = [stats]
    for step in range(1, steps + 2):
        block, gathered[-1] = lax.optimization_barrier((coming, gathered[-1]))
        other = lax.ppermute(block, "tensor", across)
        if step <= steps:
            coming = lax.ppermute(block if step < steps else half(block), AXES, along)
        gathered.append(stats_of([block, other], kept))

    mine = pl.pallas_call(
        functools.partial(pack_kernel, size),
        in_specs=[smem] + [vmem] * (len(gathered) + 3),
        out_specs=vmem,
        out_shape=jax.ShapeDtypeStruct((devices, 2, dp_count, up_to(size, 128)), jnp.float32),
        scratch_shapes=[pltpu.VMEM((2, dp_count, up_to(size, 128)), jnp.float32)],
        compiler_params=limit,
    )(place, labels.reshape(1, size), prev_scores[None, :], prev_probs[None, :], *gathered)
    every = lax.all_to_all(mine, AXES, split_axis=0, concat_axis=0, tiled=True)

    loss, scores, logs, weights = pl.pallas_call(
        functools.partial(last_kernel, tensor_count),
        in_specs=[smem, vmem, vmem],
        out_specs=[vmem] * 4,
        out_shape=[
            jax.ShapeDtypeStruct((1, size // tensor_count), jnp.float32),
            jax.ShapeDtypeStruct((1, owned), jnp.float32),
            jax.ShapeDtypeStruct((1, K), jnp.float32),
            jax.ShapeDtypeStruct((1, next_domains.shape[0]), jnp.float32),
        ],
        scratch_shapes=[pltpu.VMEM((dp_count, size), jnp.float32), pltpu.VMEM((K, 128), jnp.float32)],
        compiler_params=pltpu.CompilerParams(vmem_limit_bytes=24 << 20),
    )(place, every, next_domains[None, :])
    return (loss[0], scores[0], logs[0], weights[0])


def solution(mesh):
    placed = (
        P("dp", None),
        P(None, AXES),
        P("dp"),
        P("dp", None),
        P("dp"),
        P("dp"),
        P("dp"),
    )
    return jax.shard_map(
        body,
        mesh=mesh,
        in_specs=placed,
        out_specs=(P(AXES), P("dp"), P(), P("dp")),
        check_vma=False,
    )
```

```python
import functools
import math

import jax
import jax.numpy as jnp
from jax import lax
from jax.experimental import pallas as pl
from jax.experimental.pallas import tpu as pltpu
from jax.sharding import PartitionSpec as P

K = 64
STEP = 2000
LOW = -3.0e38
TILE = 512
KEEP = 7
NT = (((1,), (1,)), ((), ()))
AXES = ("dp", "tensor")


def exploration_rates():
    earlier = min(1.0 / K, math.sqrt(math.log(K) / (K * (STEP - 1))))
    current = min(1.0 / K, math.sqrt(math.log(K) / (K * STEP)))
    return (earlier, current)


def at_ring(place, count):
    place = lax.rem(place + count, count)
    return jnp.where(place < count // 2, 2 * place, 2 * (count - 1 - place) + 1)


def ring_place(index, count):
    half = lax.div(index, 2)
    return jnp.where(lax.rem(index, 2) == 0, half, count - 1 - half)


def slice_stats(rows, tiles, copies, vocab, wanted, vocab_offset, top, total, picked):
    count = rows.shape[0]
    full = len(tiles) - 1
    top[...] = jnp.full_like(top, LOW)
    total[...] = jnp.zeros_like(total)
    picked[...] = jnp.zeros_like(picked)
    lane = lax.broadcasted_iota(jnp.int32, (count, 128), 1)
    wanted = jnp.broadcast_to(wanted, (count, 128)) - vocab_offset - lane
    for tile in [full] + list(range(full)):
        start = tile * TILE
        if tile in copies:
            copies[tile].wait()
        logits = lax.dot_general(rows, tiles[tile][...], NT, preferred_element_type=jnp.float32)
        parts = []
        chosen = picked[...]
        for i in range(start, min(start + TILE, vocab), 128):
            part = logits[:, i - start : i - start + 128]
            if i + 128 > vocab:
                part = jnp.where(lane < vocab - i, part, LOW)
                chosen = chosen + jnp.where((wanted == i) & (lane < vocab - i), part, 0.0)
            else:
                chosen = chosen + jnp.where(wanted == i, part, 0.0)
            parts.append(part)
        picked[...] = chosen
        before = top[...]
        now = before
        for part in parts:
            now = jnp.maximum(now, part)
        added = total[...] * jnp.exp(before - now)
        for part in parts:
            added = added + jnp.exp(part - now)
        top[...] = now
        total[...] = added
    largest = jnp.max(top[...], axis=1, keepdims=True)
    summed = jnp.sum(total[...] * jnp.exp(top[...] - largest), axis=1, keepdims=True)
    pick = jnp.sum(picked[...], axis=1, keepdims=True)
    both = jnp.where(lane == 0, largest + jnp.log(summed), pick)
    if count % 128:
        both = jnp.concatenate([both, jnp.zeros((-count % 128, 128), jnp.float32)], axis=0)
    return jnp.transpose(both)[:8]


def column_from(row):
    size = row.shape[1]
    same = lax.broadcasted_iota(jnp.int32, (size, size), 0) == lax.broadcasted_iota(jnp.int32, (size, size), 1)
    return jnp.sum(jnp.where(same, row, 0), axis=1, keepdims=True)


def offset_of(place, tensor_count, vocab):
    return (place[0] * tensor_count + place[1]) * vocab


def start_copies(weight, tiles, arrived, first):
    copies = {}
    for i in range(first, first + len(tiles)):
        copies[i] = pltpu.make_async_copy(weight.at[pl.ds(i * TILE, TILE), :], tiles[i - first], arrived.at[i - first])
        copies[i].start()
    return copies


def first_kernel(tensor_count, keep, place, rows, target, ending, weight, out, *rest):
    vocab, width = weight.shape
    full = (vocab - 1) // TILE
    kept, rest = rest[: keep + 1], rest[keep + 1 :]
    streamed, rest = rest[: full - keep], rest[full - keep :]
    tiles = list(kept[:keep]) + list(streamed)
    copies = start_copies(weight, tiles, rest[0], 0)
    kept[keep][...] = ending[...]
    wanted = column_from(target[...])
    offset = offset_of(place, tensor_count, vocab)
    out[...] = slice_stats(rows[...], tiles + [ending], copies, vocab, wanted, offset, *rest[1:])


def pair_kernel(tensor_count, keep, place, one, two, target_one, target_two, weight, *rest):
    vocab, width = weight.shape
    full = (vocab - 1) // TILE
    kept, out, rest = rest[: keep + 1], rest[keep + 1], rest[keep + 2 :]
    streamed, rest = rest[: full - keep], rest[full - keep :]
    tiles = list(kept[:keep]) + list(streamed)
    copies = start_copies(weight, streamed, rest[0], keep)
    wanted = jnp.concatenate([column_from(target_one[...]), column_from(target_two[...])], axis=0)
    rows = jnp.concatenate([one[...], two[...]], axis=0)
    offset = offset_of(place, tensor_count, vocab)
    out[...] = slice_stats(rows, tiles + [kept[keep]], copies, vocab, wanted, offset, *rest[1:])


def half_kernel(place, block, target, out, target_out):
    size = out.shape[0]
    core = lax.rem(place[1], 2)
    out[...] = block[pl.ds(pl.multiple_of(core * size, size), size), :]
    target_out[...] = jnp.where(core == 0, target[:, :size], target[:, size:])


def table_kernel(size, place, own, *refs):
    stats, outs = refs[:-2], refs[-2:]
    half, piece = size // 2, size // 4
    core = lax.rem(place[1], 2)
    for theirs, out in enumerate(outs):
        out[...] = jnp.zeros_like(out)
        for kind in range(2):
            for step, table in enumerate(stats):
                row = 2 * step + kind
                out[row : row + 1, :size] = table[kind : kind + 1, theirs * size : (theirs + 1) * size]
            part = jnp.where(core == theirs, own[kind : kind + 1, :half], own[kind : kind + 1, half:size])
            for i in range(2):
                row = 2 * kind + i
                out[row : row + 1, size : size + piece] = part[:, i * piece : (i + 1) * piece]


def pack_kernel(size, steps, place, labels, scores, probs, mine, got, last, out, table):
    core = lax.rem(place[1], 2)
    row = lax.broadcasted_iota(jnp.int32, mine.shape, 0)
    lane = lax.broadcasted_iota(jnp.int32, mine.shape, 1)
    logs = jnp.where(lane < size, lax.rem(row, 2), row // 2) == 0
    one, two = mine[...], got[...]
    most = jnp.maximum(one, two)
    both = most + jnp.log(jnp.exp(one - most) + jnp.exp(two - most))
    table[...] = jnp.where(logs, both, one + two)
    for kind in range(2):
        rows = last[kind : kind + 1, :size]
        swapped = jnp.concatenate([rows[:, size // 2 :], rows[:, : size // 2]], axis=1)
        table[2 * steps + kind : 2 * steps + kind + 1, :size] = jnp.where(core == 0, rows, swapped)
    rest = table.shape[1] - size
    pieces = size // rest
    for i in range(pieces):
        table[4 + i : 5 + i, size:] = labels[:, i * rest : (i + 1) * rest].astype(jnp.float32)
    owned = scores.shape[1]
    table[4 + pieces : 5 + pieces, size : size + owned] = scores[...]
    table[4 + pieces : 5 + pieces, size + owned : size + 2 * owned] = probs[...]
    out[...] = jnp.broadcast_to(table[...][None], out.shape)


def row_of(column):
    size = column.shape[0]
    same = lax.broadcasted_iota(jnp.int32, (size, size), 0) == lax.broadcasted_iota(jnp.int32, (size, size), 1)
    return jnp.sum(jnp.where(same, column, 0.0), axis=0, keepdims=True)


def last_kernel(order, tensor_count, place, stats, domains, loss_out, score_out, log_out, weight_out, kept, kept_scores):
    dp_index, tensor_index = place[0], place[1]
    groups, size = kept.shape
    share = loss_out.shape[1]
    owned = score_out.shape[1]
    rest = stats.shape[2] - size
    pieces = size // rest
    piece = size // 4
    steps = groups // 2 - 1
    ring = {index: p for p, index in enumerate(order)}

    def rows_of(away, tensor, row):
        sources = [order[(ring[i] + away) % groups] * tensor_count + tensor for i in range(groups)]
        return jnp.concatenate([stats[d, row : row + 1, :size] for d in sources], axis=0)

    def own_rows(tensor, row):
        parts = []
        for i in range(groups):
            d = i * tensor_count + tensor
            parts.append(
                jnp.concatenate(
                    [stats[d + c, row + j : row + j + 1, size : size + piece] for c in range(2) for j in range(2)], axis=1
                )
            )
        return jnp.concatenate(parts, axis=0)

    tables = []
    for tensor in range(0, tensor_count, 2):
        tables.append((own_rows(tensor, 0), own_rows(tensor, 2)))
        for c in range(2):
            for step in range(1, steps + 1):
                away = step if c == 0 else -step
                tables.append(tuple(rows_of(away, tensor + c, 2 * step - 2 + kind) for kind in range(2)))
            tables.append(tuple(rows_of(steps + 1, tensor + c, 2 * steps + kind) for kind in range(2)))
    overall = functools.reduce(jnp.maximum, [logs for logs, _ in tables])
    total = sum(jnp.exp(logs - overall) for logs, _ in tables)
    loss = overall + jnp.log(total) - sum(picks for _, picks in tables)
    kept[...] = loss
    own = kept[pl.ds(dp_index, 1), :]
    picked = own[:, :share]
    for i in range(1, tensor_count):
        picked = jnp.where(tensor_index == i, own[:, i * share : (i + 1) * share], picked)
    loss_out[...] = picked
    number = lax.broadcasted_iota(jnp.int32, (K, size), 0).astype(jnp.float32)
    place_of = lax.broadcasted_iota(jnp.int32, (K, owned), 0) - lax.broadcasted_iota(jnp.int32, (K, owned), 1)
    sums = jnp.zeros((K, size), jnp.float32)
    counts = jnp.zeros((K, size), jnp.float32)
    scores = jnp.zeros((K, owned), jnp.float32)
    before = jnp.zeros((K, owned), jnp.float32)
    for i in range(groups):
        source = i * tensor_count
        label = jnp.concatenate([stats[source, 4 + j : 5 + j, size:] for j in range(pieces)], axis=1)
        match = number == label
        sums = sums + jnp.where(match, loss[i : i + 1, :], 0.0)
        counts = counts + jnp.where(match, 1.0, 0.0)
        here = place_of == i * owned
        scores = scores + jnp.where(here, stats[source, 4 + pieces : 5 + pieces, size : size + owned], 0.0)
        before = before + jnp.where(here, stats[source, 4 + pieces : 5 + pieces, size + owned : size + 2 * owned], 0.0)
    sums = jnp.sum(sums, axis=1, keepdims=True)
    counts = jnp.sum(counts, axis=1, keepdims=True)
    scores = jnp.sum(scores, axis=1, keepdims=True)
    before = jnp.sum(before, axis=1, keepdims=True)
    earlier, current = exploration_rates()
    new = current / earlier * scores + current * (sums / counts) / before
    kept_scores[...] = jnp.broadcast_to(new, kept_scores.shape)
    score_out[...] = row_of(kept_scores[pl.ds(pl.multiple_of(dp_index * owned, owned), owned), :][:, :1])
    weights = jnp.exp(new - jnp.max(new, axis=0, keepdims=True))
    probs = (1.0 - K * current) * (weights / jnp.sum(weights, axis=0, keepdims=True)) + current
    log_out[...] = row_of(jnp.log(probs))
    known = lax.broadcasted_iota(jnp.int32, (K, domains.shape[1]), 0) == domains[...]
    weight_out[...] = 1.0 / (K * jnp.sum(jnp.where(known, probs, 0.0), axis=0, keepdims=True))


def body(hidden, output_weight, targets, labels, prev_scores, prev_probs, next_domains):
    size, width = hidden.shape
    vocab = output_weight.shape[1]
    dp_count = lax.axis_size("dp")
    tensor_count = lax.axis_size("tensor")
    devices = dp_count * tensor_count
    owned = prev_scores.shape[0]
    steps = dp_count // 2 - 1
    place = jnp.stack([lax.axis_index("dp"), lax.axis_index("tensor")]).astype(jnp.int32)
    order = [2 * i for i in range(dp_count // 2)] + [2 * i + 1 for i in reversed(range(dp_count // 2))]
    along = []
    for p in range(dp_count):
        for t in range(tensor_count):
            to = order[(p + 1 - 2 * (t % 2)) % dp_count]
            along.append((order[p] * tensor_count + t, to * tensor_count + t))
    across = [(t, t ^ 1) for t in range(tensor_count)]

    smem = pl.BlockSpec(memory_space=pltpu.SMEM)
    vmem = pl.BlockSpec(memory_space=pltpu.VMEM)
    whole = pl.BlockSpec(memory_space=pl.ANY)
    fixed = lambda x: pltpu.with_memory_space_constraint(x, pltpu.VMEM)
    limit = pltpu.CompilerParams(vmem_limit_bytes=12 << 20)

    def up_to(count, unit):
        return -(-count // unit) * unit

    full = (vocab - 1) // TILE
    keep = min(KEEP, full)
    weight = output_weight.T
    tile = pltpu.VMEM((TILE, width), weight.dtype)

    def stats_of(blocks, wanted, kept):
        rows = sum(block.shape[0] for block in blocks)
        first = not kept
        table = jax.ShapeDtypeStruct((8, up_to(rows, 128)), jnp.float32)
        return pl.pallas_call(
            functools.partial(first_kernel if first else pair_kernel, tensor_count, keep),
            grid=(1,),
            in_specs=[smem]
            + [vmem] * (2 * len(blocks))
            + ([pl.BlockSpec((TILE, width), lambda i: (full, 0))] if first else [])
            + [whole]
            + [vmem] * len(kept),
            out_specs=[vmem] * (keep + 2) if first else vmem,
            out_shape=[table] + [tile] * (keep + 1) if first else table,
            scratch_shapes=[tile] * (full - keep)
            + [pltpu.SemaphoreType.DMA((full if first else max(full - keep, 1),))]
            + [pltpu.VMEM((rows, 128), jnp.float32)] * 3,
            compiler_params=pltpu.CompilerParams(vmem_limit_bytes=(10 + 4 * (full - keep) << 20)),
            cost_estimate=pl.CostEstimate(
                flops=2 * rows * width * vocab, bytes_accessed=2 * width * vocab, transcendentals=rows * vocab
            ),
        )(
            place, *[fixed(x) for x in blocks], *wanted, *([weight] if first else []), weight, *[fixed(x) for x in kept]
        )

    def half(block, wanted):
        return pl.pallas_call(
            half_kernel,
            in_specs=[smem, vmem, vmem],
            out_specs=[vmem] * 2,
            out_shape=[
                pltpu.VMEM((size // 2, width), block.dtype),
                jax.ShapeDtypeStruct((1, size // 2), wanted.dtype),
            ],
            compiler_params=limit,
        )(place, fixed(block), wanted)

    def moved(axes, way, *arrays):
        return [lax.ppermute(x, axes, way) for x in arrays]

    block, wanted = hidden, targets[None, :]
    coming = moved(AXES, along, block, wanted)
    stats, *kept = stats_of([block], [wanted], [])
    gathered = [stats]
    shape = (max(2 * steps + 2, 8), up_to(size, 128))
    for step in range(1, steps + 2):
        block, wanted, gathered[-1] = lax.optimization_barrier((*coming, gathered[-1]))
        other, wanted_other = moved("tensor", across, block, wanted)
        if step <= steps:
            coming = moved(AXES, along, *((block, wanted) if step < steps else half(block, wanted)))
        else:
            mine, theirs = pl.pallas_call(
                functools.partial(table_kernel, size),
                in_specs=[smem] + [vmem] * len(gathered),
                out_specs=[vmem] * 2,
                out_shape=[jax.ShapeDtypeStruct(shape, jnp.float32)] * 2,
                compiler_params=limit,
            )(place, *gathered)
            [got] = moved("tensor", across, theirs)
        gathered.append(stats_of([block, other], [wanted, wanted_other], kept))

    table = pl.pallas_call(
        functools.partial(pack_kernel, size, steps),
        in_specs=[smem] + [vmem] * 6,
        out_specs=vmem,
        out_shape=jax.ShapeDtypeStruct((devices, *shape), jnp.float32),
        scratch_shapes=[pltpu.VMEM(shape, jnp.float32)],
        compiler_params=limit,
    )(place, labels.reshape(1, size), prev_scores[None, :], prev_probs[None, :], mine, got, gathered[-1])
    every = lax.all_to_all(table, AXES, split_axis=0, concat_axis=0, tiled=True)

    loss, scores, logs, weights = pl.pallas_call(
        functools.partial(last_kernel, order, tensor_count),
        in_specs=[smem, vmem, vmem],
        out_specs=[vmem] * 4,
        out_shape=[
            jax.ShapeDtypeStruct((1, size // tensor_count), jnp.float32),
            jax.ShapeDtypeStruct((1, owned), jnp.float32),
            jax.ShapeDtypeStruct((1, K), jnp.float32),
            jax.ShapeDtypeStruct((1, next_domains.shape[0]), jnp.float32),
        ],
        scratch_shapes=[pltpu.VMEM((dp_count, size), jnp.float32), pltpu.VMEM((K, 128), jnp.float32)],
        compiler_params=pltpu.CompilerParams(vmem_limit_bytes=24 << 20),
    )(place, every, next_domains[None, :])
    return (loss[0], scores[0], logs[0], weights[0])


def solution(mesh):
    placed = (
        P("dp", None),
        P(None, AXES),
        P("dp"),
        P("dp", None),
        P("dp"),
        P("dp"),
        P("dp"),
    )
    return jax.shard_map(
        body,
        mesh=mesh,
        in_specs=placed,
        out_specs=(P(AXES), P("dp"), P(), P("dp")),
        check_vma=False,
    )
```

```python
import functools
import math

import jax
import jax.numpy as jnp
from jax import lax
from jax.experimental import pallas as pl
from jax.experimental.pallas import tpu as pltpu
from jax.sharding import PartitionSpec as P

K = 64
STEP = 2000
LOW = -3.0e38
TILE = 512
KEEP = 7
FEW = 256
NT = (((1,), (1,)), ((), ()))
AXES = ("dp", "tensor")


def exploration_rates():
    earlier = min(1.0 / K, math.sqrt(math.log(K) / (K * (STEP - 1))))
    current = min(1.0 / K, math.sqrt(math.log(K) / (K * STEP)))
    return (earlier, current)


def at_ring(place, count):
    place = lax.rem(place + count, count)
    return jnp.where(place < count // 2, 2 * place, 2 * (count - 1 - place) + 1)


def ring_place(index, count):
    half = lax.div(index, 2)
    return jnp.where(lax.rem(index, 2) == 0, half, count - 1 - half)


def slice_stats(rows, tiles, copies, vocab, wanted, vocab_offset, top, total, picked):
    count = rows.shape[0]
    full = len(tiles) - 1
    top[...] = jnp.full_like(top, LOW)
    total[...] = jnp.zeros_like(total)
    picked[...] = jnp.zeros_like(picked)
    lane = lax.broadcasted_iota(jnp.int32, (count, 128), 1)
    wanted = jnp.broadcast_to(wanted, (count, 128)) - vocab_offset - lane
    for tile in [full] + list(range(full)):
        start = tile * TILE
        if tile in copies:
            copies[tile].wait()
        logits = lax.dot_general(rows, tiles[tile][...], NT, preferred_element_type=jnp.float32)
        parts = []
        chosen = picked[...]
        for i in range(start, min(start + TILE, vocab), 128):
            part = logits[:, i - start : i - start + 128]
            if i + 128 > vocab:
                part = jnp.where(lane < vocab - i, part, LOW)
                chosen = chosen + jnp.where((wanted == i) & (lane < vocab - i), part, 0.0)
            else:
                chosen = chosen + jnp.where(wanted == i, part, 0.0)
            parts.append(part)
        picked[...] = chosen
        before = top[...]
        now = before
        for part in parts:
            now = jnp.maximum(now, part)
        added = total[...] * jnp.exp(before - now)
        for part in parts:
            added = added + jnp.exp(part - now)
        top[...] = now
        total[...] = added
    largest = jnp.max(top[...], axis=1, keepdims=True)
    summed = jnp.sum(total[...] * jnp.exp(top[...] - largest), axis=1, keepdims=True)
    pick = jnp.sum(picked[...], axis=1, keepdims=True)
    both = jnp.where(lane == 0, largest + jnp.log(summed), pick)
    if count % 128:
        both = jnp.concatenate([both, jnp.zeros((-count % 128, 128), jnp.float32)], axis=0)
    return jnp.transpose(both)[:8]


def few_stats(rows, tiles, vocab, wanted, vocab_offset, top, total, picked):
    count = rows.shape[0]
    top[...] = jnp.full_like(top, LOW)
    total[...] = jnp.zeros_like(total)
    picked[...] = jnp.zeros_like(picked)
    for tile in [len(tiles) - 1] + list(range(len(tiles) - 1)):
        start = tile * TILE
        valid = min(TILE, vocab - start)
        logits = lax.dot_general(tiles[tile][...], rows, NT, preferred_element_type=jnp.float32)
        number = lax.broadcasted_iota(jnp.int32, logits.shape, 0)
        found = jnp.where(number == wanted - vocab_offset - start, logits, 0.0)
        if valid < TILE:
            found = jnp.where(number < valid, found, 0.0)
            logits = jnp.where(number < valid, logits, LOW)
        logits = logits.reshape(TILE // 8, 8, count)
        picked[...] += jnp.sum(found.reshape(TILE // 8, 8, count), axis=0)
        before = top[...]
        now = jnp.maximum(before, jnp.max(logits, axis=0))
        total[...] = total[...] * jnp.exp(before - now) + jnp.sum(jnp.exp(logits - now[None]), axis=0)
        top[...] = now
    largest = jnp.max(top[...], axis=0, keepdims=True)
    summed = jnp.sum(total[...] * jnp.exp(top[...] - largest), axis=0, keepdims=True)
    return largest + jnp.log(summed), jnp.sum(picked[...], axis=0, keepdims=True)


def column_from(row):
    size = row.shape[1]
    same = lax.broadcasted_iota(jnp.int32, (size, size), 0) == lax.broadcasted_iota(jnp.int32, (size, size), 1)
    return jnp.sum(jnp.where(same, row, 0), axis=1, keepdims=True)


def offset_of(place, tensor_count, vocab):
    return (place[0] * tensor_count + place[1]) * vocab


def start_copies(weight, tiles, arrived, first):
    copies = {}
    for i in range(first, first + len(tiles)):
        copies[i] = pltpu.make_async_copy(weight.at[pl.ds(i * TILE, TILE), :], tiles[i - first], arrived.at[i - first])
        copies[i].start()
    return copies


def first_kernel(tensor_count, keep, place, rows, target, ending, weight, out, *rest):
    vocab, width = weight.shape
    full = (vocab - 1) // TILE
    kept, rest = rest[: keep + 1], rest[keep + 1 :]
    streamed, rest = rest[: full - keep], rest[full - keep :]
    tiles = list(kept[:keep]) + list(streamed)
    copies = start_copies(weight, tiles, rest[0], 0)
    kept[keep][...] = ending[...]
    wanted = column_from(target[...])
    offset = offset_of(place, tensor_count, vocab)
    out[...] = slice_stats(rows[...], tiles + [ending], copies, vocab, wanted, offset, *rest[1:])


def pair_kernel(tensor_count, keep, place, one, two, target_one, target_two, weight, *rest):
    vocab, width = weight.shape
    full = (vocab - 1) // TILE
    kept, out, rest = rest[: keep + 1], rest[keep + 1], rest[keep + 2 :]
    streamed, rest = rest[: full - keep], rest[full - keep :]
    tiles = list(kept[:keep]) + list(streamed)
    copies = start_copies(weight, streamed, rest[0], keep)
    tiles = tiles + [kept[keep]]
    rows = jnp.concatenate([one[...], two[...]], axis=0)
    offset = offset_of(place, tensor_count, vocab)
    if rows.shape[0] > FEW:
        wanted = jnp.concatenate([column_from(target_one[...]), column_from(target_two[...])], axis=0)
        out[...] = slice_stats(rows, tiles, copies, vocab, wanted, offset, *rest[1:])
    else:
        for copy in copies.values():
            copy.wait()
        wanted = jnp.concatenate([target_one[...], target_two[...]], axis=1)
        logs, picks = few_stats(rows, tiles, vocab, wanted, offset, *rest[1:])
        out[0:1, : rows.shape[0]] = logs
        out[1:2, : rows.shape[0]] = picks


def half_kernel(place, block, target, out, target_out):
    size = out.shape[0]
    core = lax.rem(place[1], 2)
    out[...] = block[pl.ds(pl.multiple_of(core * size, size), size), :]
    target_out[...] = jnp.where(core == 0, target[:, :size], target[:, size:])


def table_kernel(size, place, own, *refs):
    stats, outs = refs[:-2], refs[-2:]
    half, piece = size // 2, size // 4
    core = lax.rem(place[1], 2)
    for theirs, out in enumerate(outs):
        out[...] = jnp.zeros_like(out)
        for kind in range(2):
            for step, table in enumerate(stats):
                row = 2 * step + kind
                out[row : row + 1, :size] = table[kind : kind + 1, theirs * size : (theirs + 1) * size]
            part = jnp.where(core == theirs, own[kind : kind + 1, :half], own[kind : kind + 1, half:size])
            for i in range(2):
                row = 2 * kind + i
                out[row : row + 1, size : size + piece] = part[:, i * piece : (i + 1) * piece]


def pack_kernel(size, steps, place, labels, scores, probs, mine, got, last, out, table):
    core = lax.rem(place[1], 2)
    row = lax.broadcasted_iota(jnp.int32, mine.shape, 0)
    lane = lax.broadcasted_iota(jnp.int32, mine.shape, 1)
    logs = jnp.where(lane < size, lax.rem(row, 2), row // 2) == 0
    one, two = mine[...], got[...]
    most = jnp.maximum(one, two)
    both = most + jnp.log(jnp.exp(one - most) + jnp.exp(two - most))
    table[...] = jnp.where(logs, both, one + two)
    for kind in range(2):
        rows = last[kind : kind + 1, :size]
        swapped = jnp.concatenate([rows[:, size // 2 :], rows[:, : size // 2]], axis=1)
        table[2 * steps + kind : 2 * steps + kind + 1, :size] = jnp.where(core == 0, rows, swapped)
    rest = table.shape[1] - size
    pieces = size // rest
    for i in range(pieces):
        table[4 + i : 5 + i, size:] = labels[:, i * rest : (i + 1) * rest].astype(jnp.float32)
    owned = scores.shape[1]
    table[4 + pieces : 5 + pieces, size : size + owned] = scores[...]
    table[4 + pieces : 5 + pieces, size + owned : size + 2 * owned] = probs[...]
    out[...] = jnp.broadcast_to(table[...][None], out.shape)


def row_of(column):
    size = column.shape[0]
    same = lax.broadcasted_iota(jnp.int32, (size, size), 0) == lax.broadcasted_iota(jnp.int32, (size, size), 1)
    return jnp.sum(jnp.where(same, column, 0.0), axis=0, keepdims=True)


def last_kernel(order, tensor_count, place, stats, domains, loss_out, score_out, log_out, weight_out, kept, kept_scores):
    dp_index, tensor_index = place[0], place[1]
    groups, size = kept.shape
    share = loss_out.shape[1]
    owned = score_out.shape[1]
    rest = stats.shape[2] - size
    pieces = size // rest
    piece = size // 4
    steps = groups // 2 - 1
    ring = {index: p for p, index in enumerate(order)}

    def rows_of(away, tensor, row):
        sources = [order[(ring[i] + away) % groups] * tensor_count + tensor for i in range(groups)]
        return jnp.concatenate([stats[d, row : row + 1, :size] for d in sources], axis=0)

    def own_rows(tensor, row):
        parts = []
        for i in range(groups):
            d = i * tensor_count + tensor
            parts.append(
                jnp.concatenate(
                    [stats[d + c, row + j : row + j + 1, size : size + piece] for c in range(2) for j in range(2)], axis=1
                )
            )
        return jnp.concatenate(parts, axis=0)

    tables = []
    for tensor in range(0, tensor_count, 2):
        tables.append((own_rows(tensor, 0), own_rows(tensor, 2)))
        for c in range(2):
            for step in range(1, steps + 1):
                away = step if c == 0 else -step
                tables.append(tuple(rows_of(away, tensor + c, 2 * step - 2 + kind) for kind in range(2)))
            tables.append(tuple(rows_of(steps + 1, tensor + c, 2 * steps + kind) for kind in range(2)))
    overall = functools.reduce(jnp.maximum, [logs for logs, _ in tables])
    total = sum(jnp.exp(logs - overall) for logs, _ in tables)
    loss = overall + jnp.log(total) - sum(picks for _, picks in tables)
    kept[...] = loss
    own = kept[pl.ds(dp_index, 1), :]
    picked = own[:, :share]
    for i in range(1, tensor_count):
        picked = jnp.where(tensor_index == i, own[:, i * share : (i + 1) * share], picked)
    loss_out[...] = picked
    number = lax.broadcasted_iota(jnp.int32, (K, size), 0).astype(jnp.float32)
    place_of = lax.broadcasted_iota(jnp.int32, (K, owned), 0) - lax.broadcasted_iota(jnp.int32, (K, owned), 1)
    sums = jnp.zeros((K, size), jnp.float32)
    counts = jnp.zeros((K, size), jnp.float32)
    scores = jnp.zeros((K, owned), jnp.float32)
    before = jnp.zeros((K, owned), jnp.float32)
    for i in range(groups):
        source = i * tensor_count
        label = jnp.concatenate([stats[source, 4 + j : 5 + j, size:] for j in range(pieces)], axis=1)
        match = number == label
        sums = sums + jnp.where(match, loss[i : i + 1, :], 0.0)
        counts = counts + jnp.where(match, 1.0, 0.0)
        here = place_of == i * owned
        scores = scores + jnp.where(here, stats[source, 4 + pieces : 5 + pieces, size : size + owned], 0.0)
        before = before + jnp.where(here, stats[source, 4 + pieces : 5 + pieces, size + owned : size + 2 * owned], 0.0)
    sums = jnp.sum(sums, axis=1, keepdims=True)
    counts = jnp.sum(counts, axis=1, keepdims=True)
    scores = jnp.sum(scores, axis=1, keepdims=True)
    before = jnp.sum(before, axis=1, keepdims=True)
    earlier, current = exploration_rates()
    new = current / earlier * scores + current * (sums / counts) / before
    kept_scores[...] = jnp.broadcast_to(new, kept_scores.shape)
    score_out[...] = row_of(kept_scores[pl.ds(pl.multiple_of(dp_index * owned, owned), owned), :][:, :1])
    weights = jnp.exp(new - jnp.max(new, axis=0, keepdims=True))
    probs = (1.0 - K * current) * (weights / jnp.sum(weights, axis=0, keepdims=True)) + current
    log_out[...] = row_of(jnp.log(probs))
    known = lax.broadcasted_iota(jnp.int32, (K, domains.shape[1]), 0) == domains[...]
    weight_out[...] = 1.0 / (K * jnp.sum(jnp.where(known, probs, 0.0), axis=0, keepdims=True))


def body(hidden, output_weight, targets, labels, prev_scores, prev_probs, next_domains):
    size, width = hidden.shape
    vocab = output_weight.shape[1]
    dp_count = lax.axis_size("dp")
    tensor_count = lax.axis_size("tensor")
    devices = dp_count * tensor_count
    owned = prev_scores.shape[0]
    steps = dp_count // 2 - 1
    place = jnp.stack([lax.axis_index("dp"), lax.axis_index("tensor")]).astype(jnp.int32)
    order = [2 * i for i in range(dp_count // 2)] + [2 * i + 1 for i in reversed(range(dp_count // 2))]
    along = []
    for p in range(dp_count):
        for t in range(tensor_count):
            to = order[(p + 1 - 2 * (t % 2)) % dp_count]
            along.append((order[p] * tensor_count + t, to * tensor_count + t))
    across = [(t, t ^ 1) for t in range(tensor_count)]

    smem = pl.BlockSpec(memory_space=pltpu.SMEM)
    vmem = pl.BlockSpec(memory_space=pltpu.VMEM)
    whole = pl.BlockSpec(memory_space=pl.ANY)
    fixed = lambda x: pltpu.with_memory_space_constraint(x, pltpu.VMEM)
    limit = pltpu.CompilerParams(vmem_limit_bytes=12 << 20)

    def up_to(count, unit):
        return -(-count // unit) * unit

    full = (vocab - 1) // TILE
    keep = min(KEEP, full)
    weight = output_weight.T
    tile = pltpu.VMEM((TILE, width), weight.dtype)

    def stats_of(blocks, wanted, kept):
        rows = sum(block.shape[0] for block in blocks)
        first = not kept
        table = jax.ShapeDtypeStruct((8, up_to(rows, 128)), jnp.float32)
        return pl.pallas_call(
            functools.partial(first_kernel if first else pair_kernel, tensor_count, keep),
            grid=(1,),
            in_specs=[smem]
            + [vmem] * (2 * len(blocks))
            + ([pl.BlockSpec((TILE, width), lambda i: (full, 0))] if first else [])
            + [whole]
            + [vmem] * len(kept),
            out_specs=[vmem] * (keep + 2) if first else vmem,
            out_shape=[table] + [tile] * (keep + 1) if first else table,
            scratch_shapes=[tile] * (full - keep)
            + [pltpu.SemaphoreType.DMA((full if first else max(full - keep, 1),))]
            + [pltpu.VMEM((rows, 128) if first or rows > FEW else (8, rows), jnp.float32)] * 3,
            compiler_params=pltpu.CompilerParams(vmem_limit_bytes=(10 + 4 * (full - keep) << 20)),
            cost_estimate=pl.CostEstimate(
                flops=2 * rows * width * vocab, bytes_accessed=2 * width * vocab, transcendentals=rows * vocab
            ),
        )(
            place, *[fixed(x) for x in blocks], *wanted, *([weight] if first else []), weight, *[fixed(x) for x in kept]
        )

    def half(block, wanted):
        return pl.pallas_call(
            half_kernel,
            in_specs=[smem, vmem, vmem],
            out_specs=[vmem] * 2,
            out_shape=[
                pltpu.VMEM((size // 2, width), block.dtype),
                jax.ShapeDtypeStruct((1, size // 2), wanted.dtype),
            ],
            compiler_params=limit,
        )(place, fixed(block), wanted)

    def moved(axes, way, *arrays):
        return [lax.ppermute(x, axes, way) for x in arrays]

    block, wanted = hidden, targets[None, :]
    coming = moved(AXES, along, block, wanted)
    stats, *kept = stats_of([block], [wanted], [])
    gathered = [stats]
    shape = (max(2 * steps + 2, 8), up_to(size, 128))
    for step in range(1, steps + 2):
        block, wanted, gathered[-1] = lax.optimization_barrier((*coming, gathered[-1]))
        other, wanted_other = moved("tensor", across, block, wanted)
        if step <= steps:
            coming = moved(AXES, along, *((block, wanted) if step < steps else half(block, wanted)))
        else:
            mine, theirs = pl.pallas_call(
                functools.partial(table_kernel, size),
                in_specs=[smem] + [vmem] * len(gathered),
                out_specs=[vmem] * 2,
                out_shape=[jax.ShapeDtypeStruct(shape, jnp.float32)] * 2,
                compiler_params=limit,
            )(place, *gathered)
            [got] = moved("tensor", across, theirs)
        gathered.append(stats_of([block, other], [wanted, wanted_other], kept))

    table = pl.pallas_call(
        functools.partial(pack_kernel, size, steps),
        in_specs=[smem] + [vmem] * 6,
        out_specs=vmem,
        out_shape=jax.ShapeDtypeStruct((devices, *shape), jnp.float32),
        scratch_shapes=[pltpu.VMEM(shape, jnp.float32)],
        compiler_params=limit,
    )(place, labels.reshape(1, size), prev_scores[None, :], prev_probs[None, :], mine, got, gathered[-1])
    every = lax.all_to_all(table, AXES, split_axis=0, concat_axis=0, tiled=True)

    loss, scores, logs, weights = pl.pallas_call(
        functools.partial(last_kernel, order, tensor_count),
        in_specs=[smem, vmem, vmem],
        out_specs=[vmem] * 4,
        out_shape=[
            jax.ShapeDtypeStruct((1, size // tensor_count), jnp.float32),
            jax.ShapeDtypeStruct((1, owned), jnp.float32),
            jax.ShapeDtypeStruct((1, K), jnp.float32),
            jax.ShapeDtypeStruct((1, next_domains.shape[0]), jnp.float32),
        ],
        scratch_shapes=[pltpu.VMEM((dp_count, size), jnp.float32), pltpu.VMEM((K, 128), jnp.float32)],
        compiler_params=pltpu.CompilerParams(vmem_limit_bytes=24 << 20),
    )(place, every, next_domains[None, :])
    return (loss[0], scores[0], logs[0], weights[0])


def solution(mesh):
    placed = (
        P("dp", None),
        P(None, AXES),
        P("dp"),
        P("dp", None),
        P("dp"),
        P("dp"),
        P("dp"),
    )
    return jax.shard_map(
        body,
        mesh=mesh,
        in_specs=placed,
        out_specs=(P(AXES), P("dp"), P(), P("dp")),
        check_vma=False,
    )
```

```python
import functools
import math

import jax
import jax.numpy as jnp
from jax import lax
from jax.experimental import pallas as pl
from jax.experimental.pallas import tpu as pltpu
from jax.sharding import PartitionSpec as P

K = 64
STEP = 2000
LOW = -3.0e38
TILE = 512
GROUP = 2
FEW = 256
NT = (((1,), (1,)), ((), ()))
AXES = ("dp", "tensor")


def exploration_rates():
    earlier = min(1.0 / K, math.sqrt(math.log(K) / (K * (STEP - 1))))
    current = min(1.0 / K, math.sqrt(math.log(K) / (K * STEP)))
    return (earlier, current)


def at_ring(place, count):
    place = lax.rem(place + count, count)
    return jnp.where(place < count // 2, 2 * place, 2 * (count - 1 - place) + 1)


def ring_place(index, count):
    half = lax.div(index, 2)
    return jnp.where(lax.rem(index, 2) == 0, half, count - 1 - half)


def each_tile(groups, limit, visit):
    number = 0
    for place, group in enumerate(groups):
        count = group.shape[0] // TILE
        turn = limit if count % limit == 0 else count

        def body(i, carry, group=group, number=number, turn=turn, final=place == len(groups) - 1):
            for j in range(turn):
                tile = i * turn + j
                visit(group.at[pl.ds(pl.multiple_of(tile * TILE, TILE), TILE), :], number + tile, final)
            return carry

        lax.fori_loop(0, count // turn, body, 0)
        number += count


def slice_stats(rows, walk, vocab, wanted, vocab_offset, top, total, picked):
    count = rows.shape[0]
    top[...] = jnp.full_like(top, LOW)
    total[...] = jnp.zeros_like(total)
    picked[...] = jnp.zeros_like(picked)
    lane = lax.broadcasted_iota(jnp.int32, (count, 128), 1)
    wanted = jnp.broadcast_to(wanted, (count, 128)) - vocab_offset - lane

    def visit(weights, tile, final):
        logits = lax.dot_general(rows, weights[...], NT, preferred_element_type=jnp.float32)
        start = tile * TILE
        parts = []
        chosen = picked[...]
        for i in range(0, TILE, 128):
            part = logits[:, i : i + 128]
            found = wanted == start + i
            if final:
                inside = lane < vocab - start - i
                part = jnp.where(inside, part, LOW)
                found = found & inside
            chosen = chosen + jnp.where(found, part, 0.0)
            parts.append(part)
        picked[...] = chosen
        before = top[...]
        now = before
        for part in parts:
            now = jnp.maximum(now, part)
        added = total[...] * jnp.exp(before - now)
        for part in parts:
            added = added + jnp.exp(part - now)
        top[...] = now
        total[...] = added

    walk(visit)
    largest = jnp.max(top[...], axis=1, keepdims=True)
    summed = jnp.sum(total[...] * jnp.exp(top[...] - largest), axis=1, keepdims=True)
    pick = jnp.sum(picked[...], axis=1, keepdims=True)
    both = jnp.where(lane == 0, largest + jnp.log(summed), pick)
    if count % 128:
        both = jnp.concatenate([both, jnp.zeros((-count % 128, 128), jnp.float32)], axis=0)
    return jnp.transpose(both)[:8]


def few_stats(rows, walk, vocab, wanted, vocab_offset, top, total, picked):
    count = rows.shape[0]
    top[...] = jnp.full_like(top, LOW)
    total[...] = jnp.zeros_like(total)
    picked[...] = jnp.zeros_like(picked)

    def visit(weights, tile, final):
        logits = lax.dot_general(weights[...], rows, NT, preferred_element_type=jnp.float32)
        start = tile * TILE
        number = lax.broadcasted_iota(jnp.int32, logits.shape, 0)
        if final:
            logits = jnp.where(number < vocab - start, logits, LOW)
        found = number == wanted - vocab_offset - start
        if final:
            found = found & (number < vocab - start)
        found = jnp.where(found, logits, 0.0)
        logits = logits.reshape(TILE // 8, 8, count)
        picked[...] += jnp.sum(found.reshape(TILE // 8, 8, count), axis=0)
        before = top[...]
        now = jnp.maximum(before, jnp.max(logits, axis=0))
        total[...] = total[...] * jnp.exp(before - now) + jnp.sum(jnp.exp(logits - now[None]), axis=0)
        top[...] = now

    walk(visit)
    largest = jnp.max(top[...], axis=0, keepdims=True)
    summed = jnp.sum(total[...] * jnp.exp(top[...] - largest), axis=0, keepdims=True)
    return largest + jnp.log(summed), jnp.sum(picked[...], axis=0, keepdims=True)


def column_from(row):
    size = row.shape[1]
    same = lax.broadcasted_iota(jnp.int32, (size, size), 0) == lax.broadcasted_iota(jnp.int32, (size, size), 1)
    return jnp.sum(jnp.where(same, row, 0), axis=1, keepdims=True)


def offset_of(place, tensor_count, vocab):
    return (place[0] * tensor_count + place[1]) * vocab


def first_kernel(tensor_count, place, rows, target, ending, weight, out, *rest):
    vocab, width = weight.shape
    groups, arrived, scratch = rest[:-4], rest[-4], rest[-3:]
    tiles = [group.at[pl.ds(i, TILE), :] for group in groups for i in range(0, group.shape[0], TILE)]
    last = len(tiles) - 1
    copies = [
        pltpu.make_async_copy(weight.at[pl.ds(i * TILE, TILE), :], tiles[i], arrived.at[i]) for i in range(last)
    ]
    for copy in copies:
        copy.start()
    tiles[last][...] = ending[...]

    def walk(visit):
        def arriving(weights, tile, final):
            @pl.when(tile < last)
            def _():
                pltpu.make_async_copy(tiles[0], tiles[0], arrived.at[tile]).wait()

            visit(weights, tile, final)

        each_tile(groups, 1, arriving)

    wanted = column_from(target[...])
    out[...] = slice_stats(rows[...], walk, vocab, wanted, offset_of(place, tensor_count, vocab), *scratch)


def pair_kernel(tensor_count, vocab, turn, place, one, two, target_one, target_two, *rest):
    groups, out, scratch = rest[:-4], rest[-4], rest[-3:]
    rows = jnp.concatenate([one[...], two[...]], axis=0)
    offset = offset_of(place, tensor_count, vocab)
    walk = functools.partial(each_tile, groups, turn)
    if rows.shape[0] > FEW:
        wanted = jnp.concatenate([column_from(target_one[...]), column_from(target_two[...])], axis=0)
        out[...] = slice_stats(rows, walk, vocab, wanted, offset, *scratch)
    else:
        wanted = jnp.concatenate([target_one[...], target_two[...]], axis=1)
        logs, picks = few_stats(rows, walk, vocab, wanted, offset, *scratch)
        out[0:1, : rows.shape[0]] = logs
        out[1:2, : rows.shape[0]] = picks


def half_kernel(place, block, target, out, target_out):
    size = out.shape[0]
    core = lax.rem(place[1], 2)
    out[...] = block[pl.ds(pl.multiple_of(core * size, size), size), :]
    target_out[...] = jnp.where(core == 0, target[:, :size], target[:, size:])


def table_kernel(size, place, own, *refs):
    stats, outs = refs[:-2], refs[-2:]
    half, piece = size // 2, size // 4
    core = lax.rem(place[1], 2)
    for theirs, out in enumerate(outs):
        out[...] = jnp.zeros_like(out)
        for kind in range(2):
            for step, table in enumerate(stats):
                row = 2 * step + kind
                out[row : row + 1, :size] = table[kind : kind + 1, theirs * size : (theirs + 1) * size]
            part = jnp.where(core == theirs, own[kind : kind + 1, :half], own[kind : kind + 1, half:size])
            for i in range(2):
                row = 2 * kind + i
                out[row : row + 1, size : size + piece] = part[:, i * piece : (i + 1) * piece]


def pack_kernel(size, steps, place, labels, scores, probs, mine, got, last, out, table):
    core = lax.rem(place[1], 2)
    row = lax.broadcasted_iota(jnp.int32, mine.shape, 0)
    lane = lax.broadcasted_iota(jnp.int32, mine.shape, 1)
    logs = jnp.where(lane < size, lax.rem(row, 2), row // 2) == 0
    one, two = mine[...], got[...]
    most = jnp.maximum(one, two)
    both = most + jnp.log(jnp.exp(one - most) + jnp.exp(two - most))
    table[...] = jnp.where(logs, both, one + two)
    for kind in range(2):
        rows = last[kind : kind + 1, :size]
        swapped = jnp.concatenate([rows[:, size // 2 :], rows[:, : size // 2]], axis=1)
        table[2 * steps + kind : 2 * steps + kind + 1, :size] = jnp.where(core == 0, rows, swapped)
    rest = table.shape[1] - size
    pieces = size // rest
    for i in range(pieces):
        table[4 + i : 5 + i, size:] = labels[:, i * rest : (i + 1) * rest].astype(jnp.float32)
    owned = scores.shape[1]
    table[4 + pieces : 5 + pieces, size : size + owned] = scores[...]
    table[4 + pieces : 5 + pieces, size + owned : size + 2 * owned] = probs[...]
    out[...] = jnp.broadcast_to(table[...][None], out.shape)


def row_of(column):
    size = column.shape[0]
    same = lax.broadcasted_iota(jnp.int32, (size, size), 0) == lax.broadcasted_iota(jnp.int32, (size, size), 1)
    return jnp.sum(jnp.where(same, column, 0.0), axis=0, keepdims=True)


def last_kernel(order, tensor_count, place, stats, domains, loss_out, score_out, log_out, weight_out, kept, kept_scores):
    dp_index, tensor_index = place[0], place[1]
    groups, size = kept.shape
    share = loss_out.shape[1]
    owned = score_out.shape[1]
    rest = stats.shape[2] - size
    pieces = size // rest
    piece = size // 4
    steps = groups // 2 - 1
    ring = {index: p for p, index in enumerate(order)}

    def rows_of(away, tensor, row):
        sources = [order[(ring[i] + away) % groups] * tensor_count + tensor for i in range(groups)]
        return jnp.concatenate([stats[d, row : row + 1, :size] for d in sources], axis=0)

    def own_rows(tensor, row):
        parts = []
        for i in range(groups):
            d = i * tensor_count + tensor
            parts.append(
                jnp.concatenate(
                    [stats[d + c, row + j : row + j + 1, size : size + piece] for c in range(2) for j in range(2)], axis=1
                )
            )
        return jnp.concatenate(parts, axis=0)

    tables = []
    for tensor in range(0, tensor_count, 2):
        tables.append((own_rows(tensor, 0), own_rows(tensor, 2)))
        for c in range(2):
            for step in range(1, steps + 1):
                away = step if c == 0 else -step
                tables.append(tuple(rows_of(away, tensor + c, 2 * step - 2 + kind) for kind in range(2)))
            tables.append(tuple(rows_of(steps + 1, tensor + c, 2 * steps + kind) for kind in range(2)))
    overall = functools.reduce(jnp.maximum, [logs for logs, _ in tables])
    total = sum(jnp.exp(logs - overall) for logs, _ in tables)
    loss = overall + jnp.log(total) - sum(picks for _, picks in tables)
    kept[...] = loss
    own = kept[pl.ds(dp_index, 1), :]
    picked = own[:, :share]
    for i in range(1, tensor_count):
        picked = jnp.where(tensor_index == i, own[:, i * share : (i + 1) * share], picked)
    loss_out[...] = picked
    number = lax.broadcasted_iota(jnp.int32, (K, size), 0).astype(jnp.float32)
    place_of = lax.broadcasted_iota(jnp.int32, (K, owned), 0) - lax.broadcasted_iota(jnp.int32, (K, owned), 1)
    sums = jnp.zeros((K, size), jnp.float32)
    counts = jnp.zeros((K, size), jnp.float32)
    scores = jnp.zeros((K, owned), jnp.float32)
    before = jnp.zeros((K, owned), jnp.float32)
    for i in range(groups):
        source = i * tensor_count
        label = jnp.concatenate([stats[source, 4 + j : 5 + j, size:] for j in range(pieces)], axis=1)
        match = number == label
        sums = sums + jnp.where(match, loss[i : i + 1, :], 0.0)
        counts = counts + jnp.where(match, 1.0, 0.0)
        here = place_of == i * owned
        scores = scores + jnp.where(here, stats[source, 4 + pieces : 5 + pieces, size : size + owned], 0.0)
        before = before + jnp.where(here, stats[source, 4 + pieces : 5 + pieces, size + owned : size + 2 * owned], 0.0)
    sums = jnp.sum(sums, axis=1, keepdims=True)
    counts = jnp.sum(counts, axis=1, keepdims=True)
    scores = jnp.sum(scores, axis=1, keepdims=True)
    before = jnp.sum(before, axis=1, keepdims=True)
    earlier, current = exploration_rates()
    new = current / earlier * scores + current * (sums / counts) / before
    kept_scores[...] = jnp.broadcast_to(new, kept_scores.shape)
    score_out[...] = row_of(kept_scores[pl.ds(pl.multiple_of(dp_index * owned, owned), owned), :][:, :1])
    weights = jnp.exp(new - jnp.max(new, axis=0, keepdims=True))
    probs = (1.0 - K * current) * (weights / jnp.sum(weights, axis=0, keepdims=True)) + current
    log_out[...] = row_of(jnp.log(probs))
    known = lax.broadcasted_iota(jnp.int32, (K, domains.shape[1]), 0) == domains[...]
    weight_out[...] = 1.0 / (K * jnp.sum(jnp.where(known, probs, 0.0), axis=0, keepdims=True))


def body(hidden, output_weight, targets, labels, prev_scores, prev_probs, next_domains):
    size, width = hidden.shape
    vocab = output_weight.shape[1]
    dp_count = lax.axis_size("dp")
    tensor_count = lax.axis_size("tensor")
    devices = dp_count * tensor_count
    owned = prev_scores.shape[0]
    steps = dp_count // 2 - 1
    place = jnp.stack([lax.axis_index("dp"), lax.axis_index("tensor")]).astype(jnp.int32)
    order = [2 * i for i in range(dp_count // 2)] + [2 * i + 1 for i in reversed(range(dp_count // 2))]
    along = []
    for p in range(dp_count):
        for t in range(tensor_count):
            to = order[(p + 1 - 2 * (t % 2)) % dp_count]
            along.append((order[p] * tensor_count + t, to * tensor_count + t))
    across = [(t, t ^ 1) for t in range(tensor_count)]

    smem = pl.BlockSpec(memory_space=pltpu.SMEM)
    vmem = pl.BlockSpec(memory_space=pltpu.VMEM)
    whole = pl.BlockSpec(memory_space=pl.ANY)
    fixed = lambda x: pltpu.with_memory_space_constraint(x, pltpu.VMEM)
    limit = pltpu.CompilerParams(vmem_limit_bytes=12 << 20)

    def up_to(count, unit):
        return -(-count // unit) * unit

    full = (vocab - 1) // TILE
    weight = output_weight.T
    groups = [
        pltpu.VMEM((min(GROUP, full + 1 - i) * TILE, width), weight.dtype) for i in range(0, full + 1, GROUP)
    ]

    def stats_of(blocks, wanted, kept, turn=0):
        rows = sum(block.shape[0] for block in blocks)
        first = not kept
        table = jax.ShapeDtypeStruct((8, up_to(rows, 128)), jnp.float32)
        sums = pltpu.VMEM((rows, 128) if first or rows > FEW else (8, rows), jnp.float32)
        return pl.pallas_call(
            functools.partial(first_kernel, tensor_count) if first else functools.partial(pair_kernel, tensor_count, vocab, turn),
            grid=(1,),
            in_specs=[smem]
            + [vmem] * (2 * len(blocks))
            + ([pl.BlockSpec((TILE, width), lambda i: (full, 0)), whole] if first else [vmem] * len(kept)),
            out_specs=[vmem] * (1 + len(groups)) if first else vmem,
            out_shape=[table] + groups if first else table,
            scratch_shapes=([pltpu.SemaphoreType.DMA((max(full, 1),))] if first else []) + [sums] * 3,
            compiler_params=limit,
            cost_estimate=pl.CostEstimate(
                flops=2 * rows * width * vocab, bytes_accessed=2 * width * vocab, transcendentals=rows * vocab
            ),
        )(place, *[fixed(x) for x in blocks], *wanted, *([weight, weight] if first else [fixed(x) for x in kept]))

    def half(block, wanted):
        return pl.pallas_call(
            half_kernel,
            in_specs=[smem, vmem, vmem],
            out_specs=[vmem] * 2,
            out_shape=[
                pltpu.VMEM((size // 2, width), block.dtype),
                jax.ShapeDtypeStruct((1, size // 2), wanted.dtype),
            ],
            compiler_params=limit,
        )(place, fixed(block), wanted)

    def moved(axes, way, *arrays):
        return [lax.ppermute(x, axes, way) for x in arrays]

    block, wanted = hidden, targets[None, :]
    coming = moved(AXES, along, block, wanted)
    stats, *kept = stats_of([block], [wanted], [])
    gathered = [stats]
    shape = (max(2 * steps + 2, 8), up_to(size, 128))
    for step in range(1, steps + 2):
        block, wanted, gathered[-1] = lax.optimization_barrier((*coming, gathered[-1]))
        other, wanted_other = moved("tensor", across, block, wanted)
        if step <= steps:
            coming = moved(AXES, along, *((block, wanted) if step < steps else half(block, wanted)))
        else:
            mine, theirs = pl.pallas_call(
                functools.partial(table_kernel, size),
                in_specs=[smem] + [vmem] * len(gathered),
                out_specs=[vmem] * 2,
                out_shape=[jax.ShapeDtypeStruct(shape, jnp.float32)] * 2,
                compiler_params=limit,
            )(place, *gathered)
            [got] = moved("tensor", across, theirs)
        gathered.append(stats_of([block, other], [wanted, wanted_other], kept, GROUP if step == steps else 1))

    table = pl.pallas_call(
        functools.partial(pack_kernel, size, steps),
        in_specs=[smem] + [vmem] * 6,
        out_specs=vmem,
        out_shape=jax.ShapeDtypeStruct((devices, *shape), jnp.float32),
        scratch_shapes=[pltpu.VMEM(shape, jnp.float32)],
        compiler_params=limit,
    )(place, labels.reshape(1, size), prev_scores[None, :], prev_probs[None, :], mine, got, gathered[-1])
    every = lax.all_to_all(table, AXES, split_axis=0, concat_axis=0, tiled=True)

    loss, scores, logs, weights = pl.pallas_call(
        functools.partial(last_kernel, order, tensor_count),
        in_specs=[smem, vmem, vmem],
        out_specs=[vmem] * 4,
        out_shape=[
            jax.ShapeDtypeStruct((1, size // tensor_count), jnp.float32),
            jax.ShapeDtypeStruct((1, owned), jnp.float32),
            jax.ShapeDtypeStruct((1, K), jnp.float32),
            jax.ShapeDtypeStruct((1, next_domains.shape[0]), jnp.float32),
        ],
        scratch_shapes=[pltpu.VMEM((dp_count, size), jnp.float32), pltpu.VMEM((K, 128), jnp.float32)],
        compiler_params=pltpu.CompilerParams(vmem_limit_bytes=24 << 20),
    )(place, every, next_domains[None, :])
    return (loss[0], scores[0], logs[0], weights[0])


def solution(mesh):
    placed = (
        P("dp", None),
        P(None, AXES),
        P("dp"),
        P("dp", None),
        P("dp"),
        P("dp"),
        P("dp"),
    )
    return jax.shard_map(
        body,
        mesh=mesh,
        in_specs=placed,
        out_specs=(P(AXES), P("dp"), P(), P("dp")),
        check_vma=False,
    )
```

```python
import functools
import math

import jax
import jax.numpy as jnp
from jax import lax
from jax.experimental import pallas as pl
from jax.experimental.pallas import tpu as pltpu
from jax.sharding import PartitionSpec as P

K = 64
STEP = 2000
LOW = -3.0e38
TILE = 512
GROUP = 2
FEW = 256
NT = (((1,), (1,)), ((), ()))
AXES = ("dp", "tensor")


def exploration_rates():
    earlier = min(1.0 / K, math.sqrt(math.log(K) / (K * (STEP - 1))))
    current = min(1.0 / K, math.sqrt(math.log(K) / (K * STEP)))
    return (earlier, current)


def at_ring(place, count):
    place = lax.rem(place + count, count)
    return jnp.where(place < count // 2, 2 * place, 2 * (count - 1 - place) + 1)


def ring_place(index, count):
    half = lax.div(index, 2)
    return jnp.where(lax.rem(index, 2) == 0, half, count - 1 - half)


def each_tile(groups, limit, visit):
    for place, group in reversed(list(enumerate(groups))):
        number = place * GROUP
        count = group.shape[0] // TILE
        turn = limit if count % limit == 0 else count

        def body(i, carry, group=group, number=number, count=count, turn=turn, final=place == len(groups) - 1):
            for j in range(turn):
                tile = count - 1 - (i * turn + j)
                visit(group.at[pl.ds(pl.multiple_of(tile * TILE, TILE), TILE), :], number + tile, final)
            return carry

        lax.fori_loop(0, count // turn, body, 0)


def slice_stats(rows, walk, vocab, wanted, vocab_offset, top, total, picked):
    count = rows.shape[0]
    top[...] = jnp.full_like(top, LOW)
    total[...] = jnp.zeros_like(total)
    picked[...] = jnp.zeros_like(picked)
    lane = lax.broadcasted_iota(jnp.int32, (count, 128), 1)
    wanted = jnp.broadcast_to(wanted, (count, 128)) - vocab_offset - lane

    def visit(weights, tile, final):
        logits = lax.dot_general(rows, weights[...], NT, preferred_element_type=jnp.float32)
        size = weights.shape[0]
        start = tile * size
        parts = []
        chosen = picked[...]
        for i in range(0, size, 128):
            part = logits[:, i : i + 128]
            found = wanted == start + i
            if final:
                inside = lane < vocab - start - i
                part = jnp.where(inside, part, LOW)
                found = found & inside
            chosen = chosen + jnp.where(found, part, 0.0)
            parts.append(part)
        picked[...] = chosen
        before = top[...]
        now = before
        for part in parts:
            now = jnp.maximum(now, part)
        added = total[...] * jnp.exp(before - now)
        for part in parts:
            added = added + jnp.exp(part - now)
        top[...] = now
        total[...] = added

    walk(visit)
    largest = jnp.max(top[...], axis=1, keepdims=True)
    summed = jnp.sum(total[...] * jnp.exp(top[...] - largest), axis=1, keepdims=True)
    pick = jnp.sum(picked[...], axis=1, keepdims=True)
    both = jnp.where(lane == 0, largest + jnp.log(summed), pick)
    if count % 128:
        both = jnp.concatenate([both, jnp.zeros((-count % 128, 128), jnp.float32)], axis=0)
    return jnp.transpose(both)[:8]


def few_stats(rows, walk, vocab, wanted, vocab_offset, top, total, picked):
    count = rows.shape[0]
    top[...] = jnp.full_like(top, LOW)
    total[...] = jnp.zeros_like(total)
    picked[...] = jnp.zeros_like(picked)

    def visit(weights, tile, final):
        logits = lax.dot_general(weights[...], rows, NT, preferred_element_type=jnp.float32)
        size = weights.shape[0]
        start = tile * size
        number = lax.broadcasted_iota(jnp.int32, logits.shape, 0)
        if final:
            logits = jnp.where(number < vocab - start, logits, LOW)
        found = number == wanted - vocab_offset - start
        if final:
            found = found & (number < vocab - start)
        found = jnp.where(found, logits, 0.0)
        logits = logits.reshape(size // 8, 8, count)
        picked[...] += jnp.sum(found.reshape(size // 8, 8, count), axis=0)
        before = top[...]
        now = jnp.maximum(before, jnp.max(logits, axis=0))
        total[...] = total[...] * jnp.exp(before - now) + jnp.sum(jnp.exp(logits - now[None]), axis=0)
        top[...] = now

    walk(visit)
    largest = jnp.max(top[...], axis=0, keepdims=True)
    summed = jnp.sum(total[...] * jnp.exp(top[...] - largest), axis=0, keepdims=True)
    return largest + jnp.log(summed), jnp.sum(picked[...], axis=0, keepdims=True)


def column_from(row):
    size = row.shape[1]
    same = lax.broadcasted_iota(jnp.int32, (size, size), 0) == lax.broadcasted_iota(jnp.int32, (size, size), 1)
    return jnp.sum(jnp.where(same, row, 0), axis=1, keepdims=True)


def offset_of(place, tensor_count, vocab):
    return (place[0] * tensor_count + place[1]) * vocab


def first_kernel(tensor_count, place, rows, target, ending, weight, out, *rest):
    vocab, width = weight.shape
    groups, arrived, scratch = rest[:-4], rest[-4], rest[-3:]
    tiles = [group.at[pl.ds(i, TILE), :] for group in groups for i in range(0, group.shape[0], TILE)]
    last = len(tiles) - 1
    copies = [
        pltpu.make_async_copy(weight.at[pl.ds(i * TILE, TILE), :], tiles[i], arrived.at[i]) for i in range(last)
    ]
    for copy in reversed(copies):
        copy.start()
    tiles[last][...] = ending[...]

    def walk(visit):
        def arriving(weights, tile, final):
            @pl.when(tile < last)
            def _():
                pltpu.make_async_copy(tiles[0], tiles[0], arrived.at[tile]).wait()

            def half(i, carry):
                visit(weights.at[pl.ds(pl.multiple_of(i * (TILE // 2), TILE // 2), TILE // 2), :], 2 * tile + i, final)
                return carry

            lax.fori_loop(0, 2, half, 0)

        each_tile(groups, 1, arriving)

    offset = offset_of(place, tensor_count, vocab)
    if rows.shape[0] > FEW:
        out[...] = slice_stats(rows[...], walk, vocab, column_from(target[...]), offset, *scratch)
    else:
        logs, picks = few_stats(rows[...], walk, vocab, target[...], offset, *scratch)
        out[0:1, : rows.shape[0]] = logs
        out[1:2, : rows.shape[0]] = picks


def pair_kernel(tensor_count, vocab, turn, place, one, two, target_one, target_two, *rest):
    groups, out, scratch = rest[:-4], rest[-4], rest[-3:]
    rows = jnp.concatenate([one[...], two[...]], axis=0)
    offset = offset_of(place, tensor_count, vocab)
    walk = functools.partial(each_tile, groups, turn)
    if rows.shape[0] > FEW:
        wanted = jnp.concatenate([column_from(target_one[...]), column_from(target_two[...])], axis=0)
        out[...] = slice_stats(rows, walk, vocab, wanted, offset, *scratch)
    else:
        wanted = jnp.concatenate([target_one[...], target_two[...]], axis=1)
        logs, picks = few_stats(rows, walk, vocab, wanted, offset, *scratch)
        out[0:1, : rows.shape[0]] = logs
        out[1:2, : rows.shape[0]] = picks


def half_kernel(place, block, target, out, target_out):
    size = out.shape[0]
    core = lax.rem(place[1], 2)
    out[...] = block[pl.ds(pl.multiple_of(core * size, size), size), :]
    target_out[...] = jnp.where(core == 0, target[:, :size], target[:, size:])


def table_kernel(size, place, own, *refs):
    stats, outs = refs[:-2], refs[-2:]
    half, piece = size // 2, size // 4
    core = lax.rem(place[1], 2)
    for theirs, out in enumerate(outs):
        out[...] = jnp.zeros_like(out)
        for kind in range(2):
            for step, table in enumerate(stats):
                row = 2 * step + kind
                out[row : row + 1, :size] = table[kind : kind + 1, theirs * size : (theirs + 1) * size]
            part = jnp.where(core == theirs, own[kind : kind + 1, :half], own[kind : kind + 1, half:size])
            for i in range(2):
                row = 2 * kind + i
                out[row : row + 1, size : size + piece] = part[:, i * piece : (i + 1) * piece]


def pack_kernel(size, steps, place, labels, scores, probs, mine, got, last, out, table):
    core = lax.rem(place[1], 2)
    row = lax.broadcasted_iota(jnp.int32, mine.shape, 0)
    lane = lax.broadcasted_iota(jnp.int32, mine.shape, 1)
    logs = jnp.where(lane < size, lax.rem(row, 2), row // 2) == 0
    one, two = mine[...], got[...]
    most = jnp.maximum(one, two)
    both = most + jnp.log(jnp.exp(one - most) + jnp.exp(two - most))
    table[...] = jnp.where(logs, both, one + two)
    for kind in range(2):
        rows = last[kind : kind + 1, :size]
        swapped = jnp.concatenate([rows[:, size // 2 :], rows[:, : size // 2]], axis=1)
        table[2 * steps + kind : 2 * steps + kind + 1, :size] = jnp.where(core == 0, rows, swapped)
    rest = table.shape[1] - size
    pieces = size // rest
    for i in range(pieces):
        table[4 + i : 5 + i, size:] = labels[:, i * rest : (i + 1) * rest].astype(jnp.float32)
    owned = scores.shape[1]
    table[4 + pieces : 5 + pieces, size : size + owned] = scores[...]
    table[4 + pieces : 5 + pieces, size + owned : size + 2 * owned] = probs[...]
    out[...] = jnp.broadcast_to(table[...][None], out.shape)


def row_of(column):
    size = column.shape[0]
    same = lax.broadcasted_iota(jnp.int32, (size, size), 0) == lax.broadcasted_iota(jnp.int32, (size, size), 1)
    return jnp.sum(jnp.where(same, column, 0.0), axis=0, keepdims=True)


def last_kernel(order, tensor_count, place, stats, domains, loss_out, score_out, log_out, weight_out, kept, kept_scores):
    dp_index, tensor_index = place[0], place[1]
    groups, size = kept.shape
    share = loss_out.shape[1]
    owned = score_out.shape[1]
    rest = stats.shape[2] - size
    pieces = size // rest
    piece = size // 4
    steps = groups // 2 - 1
    ring = {index: p for p, index in enumerate(order)}

    def rows_of(away, tensor, row):
        sources = [order[(ring[i] + away) % groups] * tensor_count + tensor for i in range(groups)]
        return jnp.concatenate([stats[d, row : row + 1, :size] for d in sources], axis=0)

    def own_rows(tensor, row):
        parts = []
        for i in range(groups):
            d = i * tensor_count + tensor
            parts.append(
                jnp.concatenate(
                    [stats[d + c, row + j : row + j + 1, size : size + piece] for c in range(2) for j in range(2)], axis=1
                )
            )
        return jnp.concatenate(parts, axis=0)

    tables = []
    for tensor in range(0, tensor_count, 2):
        tables.append((own_rows(tensor, 0), own_rows(tensor, 2)))
        for c in range(2):
            for step in range(1, steps + 1):
                away = step if c == 0 else -step
                tables.append(tuple(rows_of(away, tensor + c, 2 * step - 2 + kind) for kind in range(2)))
            tables.append(tuple(rows_of(steps + 1, tensor + c, 2 * steps + kind) for kind in range(2)))
    overall = functools.reduce(jnp.maximum, [logs for logs, _ in tables])
    total = sum(jnp.exp(logs - overall) for logs, _ in tables)
    loss = overall + jnp.log(total) - sum(picks for _, picks in tables)
    kept[...] = loss
    own = kept[pl.ds(dp_index, 1), :]
    picked = own[:, :share]
    for i in range(1, tensor_count):
        picked = jnp.where(tensor_index == i, own[:, i * share : (i + 1) * share], picked)
    loss_out[...] = picked
    number = lax.broadcasted_iota(jnp.int32, (K, size), 0).astype(jnp.float32)
    place_of = lax.broadcasted_iota(jnp.int32, (K, owned), 0) - lax.broadcasted_iota(jnp.int32, (K, owned), 1)
    sums = jnp.zeros((K, size), jnp.float32)
    counts = jnp.zeros((K, size), jnp.float32)
    scores = jnp.zeros((K, owned), jnp.float32)
    before = jnp.zeros((K, owned), jnp.float32)
    for i in range(groups):
        source = i * tensor_count
        label = jnp.concatenate([stats[source, 4 + j : 5 + j, size:] for j in range(pieces)], axis=1)
        match = number == label
        sums = sums + jnp.where(match, loss[i : i + 1, :], 0.0)
        counts = counts + jnp.where(match, 1.0, 0.0)
        here = place_of == i * owned
        scores = scores + jnp.where(here, stats[source, 4 + pieces : 5 + pieces, size : size + owned], 0.0)
        before = before + jnp.where(here, stats[source, 4 + pieces : 5 + pieces, size + owned : size + 2 * owned], 0.0)
    sums = jnp.sum(sums, axis=1, keepdims=True)
    counts = jnp.sum(counts, axis=1, keepdims=True)
    scores = jnp.sum(scores, axis=1, keepdims=True)
    before = jnp.sum(before, axis=1, keepdims=True)
    earlier, current = exploration_rates()
    new = current / earlier * scores + current * (sums / counts) / before
    kept_scores[...] = jnp.broadcast_to(new, kept_scores.shape)
    score_out[...] = row_of(kept_scores[pl.ds(pl.multiple_of(dp_index * owned, owned), owned), :][:, :1])
    weights = jnp.exp(new - jnp.max(new, axis=0, keepdims=True))
    probs = (1.0 - K * current) * (weights / jnp.sum(weights, axis=0, keepdims=True)) + current
    log_out[...] = row_of(jnp.log(probs))
    known = lax.broadcasted_iota(jnp.int32, (K, domains.shape[1]), 0) == domains[...]
    weight_out[...] = 1.0 / (K * jnp.sum(jnp.where(known, probs, 0.0), axis=0, keepdims=True))


def body(hidden, output_weight, targets, labels, prev_scores, prev_probs, next_domains):
    size, width = hidden.shape
    vocab = output_weight.shape[1]
    dp_count = lax.axis_size("dp")
    tensor_count = lax.axis_size("tensor")
    devices = dp_count * tensor_count
    owned = prev_scores.shape[0]
    steps = dp_count // 2 - 1
    place = jnp.stack([lax.axis_index("dp"), lax.axis_index("tensor")]).astype(jnp.int32)
    order = [2 * i for i in range(dp_count // 2)] + [2 * i + 1 for i in reversed(range(dp_count // 2))]
    along = []
    for p in range(dp_count):
        for t in range(tensor_count):
            to = order[(p + 1 - 2 * (t % 2)) % dp_count]
            along.append((order[p] * tensor_count + t, to * tensor_count + t))
    across = [(t, t ^ 1) for t in range(tensor_count)]

    smem = pl.BlockSpec(memory_space=pltpu.SMEM)
    vmem = pl.BlockSpec(memory_space=pltpu.VMEM)
    whole = pl.BlockSpec(memory_space=pl.ANY)
    fixed = lambda x: pltpu.with_memory_space_constraint(x, pltpu.VMEM)
    limit = pltpu.CompilerParams(vmem_limit_bytes=12 << 20)

    def up_to(count, unit):
        return -(-count // unit) * unit

    full = (vocab - 1) // TILE
    weight = output_weight.T
    groups = [
        pltpu.VMEM((min(GROUP, full + 1 - i) * TILE, width), weight.dtype) for i in range(0, full + 1, GROUP)
    ]

    def stats_of(blocks, wanted, kept, turn=0):
        rows = sum(block.shape[0] for block in blocks)
        first = not kept
        table = jax.ShapeDtypeStruct((8, up_to(rows, 128)), jnp.float32)
        sums = pltpu.VMEM((rows, 128) if rows > FEW else (8, rows), jnp.float32)
        return pl.pallas_call(
            functools.partial(first_kernel, tensor_count) if first else functools.partial(pair_kernel, tensor_count, vocab, turn),
            grid=(1,),
            in_specs=[smem]
            + [vmem] * (2 * len(blocks))
            + ([pl.BlockSpec((TILE, width), lambda i: (full, 0)), whole] if first else [vmem] * len(kept)),
            out_specs=[vmem] * (1 + len(groups)) if first else vmem,
            out_shape=[table] + groups if first else table,
            scratch_shapes=([pltpu.SemaphoreType.DMA((max(full, 1),))] if first else []) + [sums] * 3,
            compiler_params=limit,
            cost_estimate=pl.CostEstimate(
                flops=2 * rows * width * vocab, bytes_accessed=2 * width * vocab, transcendentals=rows * vocab
            ),
        )(place, *[fixed(x) for x in blocks], *wanted, *([weight, weight] if first else [fixed(x) for x in kept]))

    def half(block, wanted):
        return pl.pallas_call(
            half_kernel,
            in_specs=[smem, vmem, vmem],
            out_specs=[vmem] * 2,
            out_shape=[
                pltpu.VMEM((size // 2, width), block.dtype),
                jax.ShapeDtypeStruct((1, size // 2), wanted.dtype),
            ],
            compiler_params=limit,
        )(place, fixed(block), wanted)

    def moved(axes, way, *arrays):
        return [lax.ppermute(x, axes, way) for x in arrays]

    block, wanted = hidden, targets[None, :]
    coming = moved(AXES, along, block, wanted)
    stats, *kept = stats_of([block], [wanted], [])
    gathered = [stats]
    shape = (max(2 * steps + 2, 8), up_to(size, 128))
    for step in range(1, steps + 2):
        block, wanted, gathered[-1] = lax.optimization_barrier((*coming, gathered[-1]))
        other, wanted_other = moved("tensor", across, block, wanted)
        if step <= steps:
            coming = moved(AXES, along, *((block, wanted) if step < steps else half(block, wanted)))
        else:
            mine, theirs = pl.pallas_call(
                functools.partial(table_kernel, size),
                in_specs=[smem] + [vmem] * len(gathered),
                out_specs=[vmem] * 2,
                out_shape=[jax.ShapeDtypeStruct(shape, jnp.float32)] * 2,
                compiler_params=limit,
            )(place, *gathered)
            [got] = moved("tensor", across, theirs)
        gathered.append(stats_of([block, other], [wanted, wanted_other], kept, GROUP if step >= steps else 1))

    table = pl.pallas_call(
        functools.partial(pack_kernel, size, steps),
        in_specs=[smem] + [vmem] * 6,
        out_specs=vmem,
        out_shape=jax.ShapeDtypeStruct((devices, *shape), jnp.float32),
        scratch_shapes=[pltpu.VMEM(shape, jnp.float32)],
        compiler_params=limit,
    )(place, labels.reshape(1, size), prev_scores[None, :], prev_probs[None, :], mine, got, gathered[-1])
    every = lax.all_to_all(table, AXES, split_axis=0, concat_axis=0, tiled=True)

    loss, scores, logs, weights = pl.pallas_call(
        functools.partial(last_kernel, order, tensor_count),
        in_specs=[smem, vmem, vmem],
        out_specs=[vmem] * 4,
        out_shape=[
            jax.ShapeDtypeStruct((1, size // tensor_count), jnp.float32),
            jax.ShapeDtypeStruct((1, owned), jnp.float32),
            jax.ShapeDtypeStruct((1, K), jnp.float32),
            jax.ShapeDtypeStruct((1, next_domains.shape[0]), jnp.float32),
        ],
        scratch_shapes=[pltpu.VMEM((dp_count, size), jnp.float32), pltpu.VMEM((K, 128), jnp.float32)],
        compiler_params=pltpu.CompilerParams(vmem_limit_bytes=24 << 20),
    )(place, every, next_domains[None, :])
    return (loss[0], scores[0], logs[0], weights[0])


def solution(mesh):
    placed = (
        P("dp", None),
        P(None, AXES),
        P("dp"),
        P("dp", None),
        P("dp"),
        P("dp"),
        P("dp"),
    )
    return jax.shard_map(
        body,
        mesh=mesh,
        in_specs=placed,
        out_specs=(P(AXES), P("dp"), P(), P("dp")),
        check_vma=False,
    )
```
